32 devices in a mesh: grp: 2 (over y), wide: 8 (over z, x), narrow: 2 (over core).
Axes of the slice: x: 2, y: 2, z: 4, core: 2. Of those that a mesh axis runs over, the one named last changes fastest.
Arguments:
- tile_hidden: bfloat16 [32, 64, 1024], P(('grp', 'wide')), parts along dimension 0, may hold values from -6 to 6
- cached_rows: bfloat16 [2048, 2048], P(('grp', 'wide'), 'narrow'), parts along dimension 0, may hold values from -5 to 5
- tile_image: int32 [32], P(('grp', 'wide')), parts along dimension 0, may hold values from 0 to 4095, as said below
- cache_ids: int32 [128], P('grp'), parts along dimension 0, may hold values from 0 to 4095, as said below
- adapter_weight: bfloat16 [1024, 2048], P('wide', 'narrow'), may hold values from -0.1875 to 0.1875
- routes: int32 [2048, 6], P(('grp', 'wide')), parts along dimension 0, may hold values from 0 to 63, all different within a row; in each aligned block of 128 rows (0 to 127, 128 to 255, ...) at most 16 rows name the same one
- route_gates: float32 [2048, 6], P(('grp', 'wide')), parts along dimension 0, may hold values from 0.03 to 0.4
- gate_up: bfloat16 [128, 2048, 2, 512], P('wide', 'narrow'), may hold values from -0.125 to 0.125
- expert_down: bfloat16 [128, 512, 2048], P('wide', None, 'narrow'), may hold values from -0.1875 to 0.1875
Outputs:
- expert_mix: bfloat16 [2048, 2048], P(('grp', 'wide'), 'narrow'), parts along dimension 0
The draws below stay inside these ranges and needn't reach their ends.
There are 2 independent parts, one for each index of `grp`. The reference program is written for one: setup_inputs(seed, part) draws one part's arguments, and reference() takes and returns one part's arrays. A program takes and returns all parts, laid end to end along the dimension named above; an argument that names none is the same for every part. Nothing has to cross between parts.
Inputs may be any that keep to these rules, and one draw needn't show every extreme that they name: `tile_image`: slot s belongs to chip s // 2. A slot misses the cache when its image id is not in cache_ids. Chips w and w + 4 together have at most 2 missed slots, and in every draw some chip misses all 2 of its slots. `cache_ids`: the ids are distinct. `routes`: within the rows of one chip (128 tokens), no expert is named by more than 16 rows, and in every draw some expert is named by exactly 16 rows of some chip.
All inputs are finite; a program needn't handle non-finite values.
Results may differ from the reference program's by a relative error of at most 0.018.
Values may be sent and summed in bfloat16 or wider, within the bound.
No kernel may reach another device: no remote copies, remote signals or barrier semaphores. Data moves between devices by JAX's collectives and lax.ppermute only.
A program may use at most 192 MiB of HBM per device.

```python
import math
import jax
import jax.numpy as jnp
import numpy as np
from jax import lax

D = 2048
EXPERTS = 64
TOP = 6
AH = 1024
FE = 1024
FH = 512
CAP = 16
TILE_ROWS = 64
SLOT_DEV = 2
CACHE = 64
TOK_DEV = 128
TOKENS = 1024
TILES = 16
HALVES = 128
N_WIDE = 8


id_space = 4096


def missing_slots(key):
    chip_count = TILES // SLOT_DEV
    pair_count = chip_count // 2
    pair_index = jnp.arange(pair_count, dtype=jnp.int32)
    forced = jax.random.randint(jax.random.fold_in(key, 1), (), 0, pair_count)
    lower_side = jax.random.randint(jax.random.fold_in(key, 2), (), 0, 2)
    totals = jax.random.randint(jax.random.fold_in(key, 3), (pair_count,), 0, SLOT_DEV + 1)
    totals = jnp.where(pair_index == forced, SLOT_DEV, totals)
    lower_load = jax.random.randint(jax.random.fold_in(key, 4), (pair_count,), 0, totals + 1)
    lower_load = jnp.where(pair_index == forced, lower_side * SLOT_DEV, lower_load)
    loads = jnp.concatenate([lower_load, totals - lower_load])
    scores = jax.random.randint(jax.random.fold_in(key, 5), (chip_count, SLOT_DEV), 0, 1 << 24)
    places = jnp.argsort(jnp.argsort(scores, axis=1, stable=True), axis=1, stable=True)
    return (places < loads[:, None]).reshape(-1)


def image_tables(key):
    missing = missing_slots(jax.random.fold_in(key, 7))
    shuffled = jax.random.permutation(jax.random.fold_in(key, 8), id_space).astype(jnp.int32)
    cached = shuffled[:CACHE]
    absent = shuffled[CACHE:]
    hit_pick = jax.random.randint(jax.random.fold_in(key, 9), (TILES,), 0, CACHE)
    miss_pick = jax.random.randint(jax.random.fold_in(key, 10), (TILES,), 0, id_space - CACHE)
    images = jnp.where(missing, absent[miss_pick], cached[hit_pick]).astype(jnp.int32)
    return (images, cached)


def draw_tile_image(key, part):
    images, cached = image_tables(key)
    return images


def draw_cache_ids(key, part):
    images, cached = image_tables(key)
    return cached


def levels(key, dims, pieces, smallest, high):
    gain = 1.0
    for position, parts in pieces:
        heights = jax.random.uniform(jax.random.fold_in(jax.random.fold_in(key, 6), position), (parts,), jnp.float32, smallest / len(pieces), high / len(pieces))
        gain = gain * jnp.repeat(jnp.exp(heights), dims[position] // parts).reshape((-1,) + (1,) * (len(dims) - 1 - position))
    return gain


def assign_block(rng, own, number, rows, count, top, limit, lean):
    sequence = jax.random.permutation(rng, count)
    packed, usual = portions_of(count, rows * top, limit, lean, True), portions_of(count, rows * top, limit, lean, False)
    places = jnp.arange(count)

    def named(tallies, turn):
        used = int((tallies > 0).sum())
        fixed = max(1, used // 4)
        passed = fixed + (places - fixed + turn * (used - fixed)) % max(1, count - fixed)
        return jnp.zeros((count,), jnp.int32).at[sequence[jnp.where(places < fixed, places, passed)]].set(jnp.asarray(tallies, jnp.int32))

    tallies = jnp.where(number % 4 == 0, named(packed, number // 4), named(usual, number - number // 4 - 1))
    mixed = jax.random.permutation(jax.random.fold_in(own, 3), count)
    donor, receiver = mixed[0:count // 2 * 2:2], mixed[1:count // 2 * 2:2]
    margin = jnp.minimum(tallies[donor] - 1, limit - tallies[receiver]) // 2
    margin = jnp.where((donor == sequence[0]) | (receiver == sequence[0]) | (tallies[receiver] == 0), 0, jnp.maximum(margin, 0))
    passed = jax.random.randint(jax.random.fold_in(own, 4), (count // 2,), 0, 1 << 20) % (margin + 1)
    tallies = tallies.at[donor].add(-passed).at[receiver].add(passed)
    labels = jnp.searchsorted(jnp.cumsum(tallies), jnp.arange(rows * top), side="right").astype(jnp.int32)
    grid = labels.reshape(top, rows).T
    grid = grid[jax.random.permutation(jax.random.fold_in(own, 1), rows)]
    turn = jax.random.randint(jax.random.fold_in(own, 2), (rows, 1), 0, top)
    return jnp.take_along_axis(grid, (jnp.arange(top)[None, :] + turn) % top, axis=1)


def portions_of(number_of, total, bound, lean, full):
    weights = [(1 << 20) // math.isqrt(grade ** lean) + 1 for grade in range(1, number_of + 1)]
    largest = bound if full else min(bound, max(-(-total // number_of), total * weights[0] // sum(weights)))
    least = 1 if total - largest >= number_of - 1 else 0
    holding, spare = [largest] + [least] * (number_of - 1), total - largest - least * (number_of - 1)
    while spare > 0:
        movable = [i for i in range(1, number_of) if holding[i] < largest] or [i for i in range(1, number_of) if holding[i] < bound]
        mass, left = sum([weights[i] for i in movable]), spare
        for i in movable:
            addition = min(bound - holding[i], max(1, left * weights[i] // mass), spare)
            holding[i] = holding[i] + addition
            spare = spare - addition
    return np.array(holding)


def noise(rng, extent, deviation, bound, shards=(), held_as=jnp.bfloat16):
    result = deviation * jax.random.normal(rng, extent, jnp.float32)
    if shards:
        result = result * levels(rng, extent, shards, -0.22, 0.18)
    return jnp.clip(result, -bound, bound).astype(held_as)


def setup_inputs(seed: int = 0, part: int = 0) -> dict:
    keys = jax.random.split(jax.random.key(seed), 10)
    part_splits = jax.random.split(jax.random.fold_in(keys[9], part), 10)
    tile_hidden = noise(part_splits[0], (TILES, TILE_ROWS, AH), 1.0, 6.0, ((0, 8),))
    cached_rows = noise(part_splits[1], (TOKENS, D), 0.7, 5.0, ((0, 8), (1, 2)))
    tile_image = draw_tile_image(jax.random.fold_in(jax.random.fold_in(keys[9], part), 71), part)
    cache_ids = draw_cache_ids(jax.random.fold_in(jax.random.fold_in(keys[9], part), 71), part)
    adapter_weight = noise(keys[4], (AH, D), AH ** -0.5, 0.1875, ((0, 8), (1, 2)))
    routes_keys = jax.random.split(jax.random.fold_in(part_splits[5], 1), TOKENS // TOK_DEV)
    routes_turns = jax.random.permutation(jax.random.fold_in(part_splits[5], 3), TOKENS // TOK_DEV)
    routes = jax.vmap(lambda own, number: assign_block(jax.random.fold_in(part_splits[5], 2), own, number, TOK_DEV, EXPERTS, TOP, CAP, 2))(routes_keys, routes_turns).reshape((TOKENS, TOP))
    route_gates = jnp.clip(jnp.exp(math.log(0.4) - 2.5902672 * jax.random.uniform(part_splits[6], (TOKENS, TOP), jnp.float32) ** levels(part_splits[6], (TOKENS, TOP), ((0, 8),), -0.2, 0.2)), 0.03, 0.4)
    gate_up = noise(keys[7], (HALVES, D, 2, FH), D ** -0.5, 0.125, ((0, 8), (1, 2)))
    expert_down = noise(keys[8], (HALVES, FH, D), FE ** -0.5, 0.1875, ((0, 8), (2, 2)))
    return dict(tile_hidden=tile_hidden, cached_rows=cached_rows, tile_image=tile_image, cache_ids=cache_ids, adapter_weight=adapter_weight, routes=routes, route_gates=route_gates, gate_up=gate_up, expert_down=expert_down)


def round_keep(values):
    return lax.optimization_barrier(values.astype(jnp.bfloat16)).astype(jnp.float32)


def reference(tile_hidden, cached_rows, tile_image, cache_ids, adapter_weight, routes, route_gates, gate_up, expert_down):
    tile_count, tile_rows, adapt_width = tile_hidden.shape
    cache_hit = jnp.any(tile_image[:, None] == cache_ids[None, :], axis=1)
    active = jax.nn.gelu(tile_hidden.astype(jnp.float32), approximate=False).astype(jnp.bfloat16)
    encoded = jnp.dot(active.reshape(tile_count * tile_rows, adapt_width), adapter_weight, preferred_element_type=jnp.float32).astype(jnp.bfloat16)
    hit_rows = jnp.repeat(cache_hit, tile_rows)
    tokens_in = jnp.where(hit_rows[:, None], cached_rows, encoded)
    expert_flat = routes.reshape(-1).astype(jnp.int32)
    gate_flat = route_gates.reshape(-1)
    most_rows = N_WIDE * CAP
    sorted_pairs = jnp.argsort(expert_flat, stable=True).astype(jnp.int32)
    sorted_pairs = jnp.concatenate([sorted_pairs, jnp.zeros((most_rows,), jnp.int32)])
    experts_all = jnp.arange(EXPERTS, dtype=jnp.int32)
    counts = jnp.sum((expert_flat[:, None] == experts_all[None, :]).astype(jnp.int32), axis=0)
    starts = (jnp.cumsum(counts) - counts).astype(jnp.int32)
    half_width = D // 2
    inner_width = gate_up.shape[3]
    weights_in = gate_up.astype(jnp.float32).reshape(EXPERTS, 2, D, 2 * inner_width)
    weights_out = expert_down.astype(jnp.float32).reshape(EXPERTS, 2, inner_width, D)
    tokens_wide = tokens_in.astype(jnp.float32)
    positions = jnp.arange(most_rows, dtype=jnp.int32)
    highest = lax.Precision.HIGHEST

    def one_expert(running, expert):
        chosen = lax.dynamic_slice_in_dim(sorted_pairs, starts[expert].astype(jnp.int32), most_rows)
        is_valid = positions < counts[expert]
        owners = chosen // TOP
        rows_in = tokens_wide[owners]
        weight = jnp.where(is_valid, gate_flat[chosen], jnp.zeros_like(gate_flat[chosen]))
        summed = jnp.zeros((most_rows, D), jnp.float32)
        for halfpart in range(2):
            matrix = weights_in[expert, halfpart]
            low_part = jnp.dot(rows_in[:, :half_width], matrix[:half_width], precision=highest)
            high_part = jnp.dot(rows_in[:, half_width:], matrix[half_width:], precision=highest)
            preact = round_keep(low_part) + round_keep(high_part)
            hidden = round_keep(jax.nn.silu(preact[:, :inner_width]) * preact[:, inner_width:])
            summed = summed + round_keep(jnp.dot(hidden, weights_out[expert, halfpart], precision=highest))
        summed = round_keep(summed)
        return running.at[owners].add(weight[:, None] * summed), None

    initial = jnp.zeros((TOKENS, D), jnp.float32)
    final, unused = lax.scan(one_expert, initial, experts_all)
    return final.astype(jnp.bfloat16)
```

```python
import functools

import jax
import jax.numpy as jnp
from jax import lax
from jax.experimental import pallas as pl
from jax.experimental.pallas import tpu as pltpu
from jax.sharding import PartitionSpec as P

EXPERTS = 64
TOP = 6
CAP = 16
F32 = jnp.float32
BF16 = jnp.bfloat16
RING = (0, 2, 4, 6, 7, 5, 3, 1)
NR = 8
VMEM_LIMIT = 48 << 20
ANY = pl.BlockSpec(memory_space=pl.ANY)
VM = pl.BlockSpec(memory_space=pltpu.VMEM)
SM = pl.BlockSpec(memory_space=pltpu.SMEM)


def activate(tiles):
    return jax.nn.gelu(tiles.astype(F32), approximate=False).astype(BF16)


def round_keep(values):
    return lax.optimization_barrier(values.astype(BF16)).astype(F32)


def on_device_plain(
    tile_hidden, cached_rows, tile_image, cache_ids, adapter_weight, routes, route_gates, gate_up, expert_down
):
    slot_count, tile_rows, adapt_width = tile_hidden.shape
    half_width = cached_rows.shape[1]
    cache_hit = jnp.any(tile_image[:, None] == cache_ids[None, :], axis=1)
    whole_weight = lax.all_gather(adapter_weight, "wide", axis=0, tiled=True)
    active = activate(tile_hidden).reshape(slot_count * tile_rows, adapt_width)
    encoded = jnp.dot(active, whole_weight, preferred_element_type=F32).astype(BF16)
    token_count = slot_count * tile_rows
    hit_rows = jnp.repeat(cache_hit, tile_rows)
    tokens_in = jnp.where(hit_rows[:, None], cached_rows, encoded)
    expert_flat = routes.reshape(-1)
    pair_count = expert_flat.shape[0]
    onehot = (expert_flat[:, None] == jnp.arange(EXPERTS, dtype=jnp.int32)[None, :]).astype(jnp.int32)
    earlier = jnp.cumsum(onehot, axis=0) - onehot
    slot_index = jnp.sum(earlier * onehot, axis=1)
    target = expert_flat * CAP + slot_index
    owner_table = (
        jnp.full((EXPERTS * CAP,), token_count, jnp.int32)
        .at[target]
        .set(jnp.arange(pair_count, dtype=jnp.int32) // TOP)
    )
    padded_tokens = jnp.concatenate([tokens_in, jnp.zeros((1, half_width), BF16)])
    expert_rows = padded_tokens[owner_table].reshape(EXPERTS, CAP, half_width)
    local_halves = gate_up.shape[0]
    outgoing = jnp.broadcast_to(expert_rows[:, None], (EXPERTS, 2, CAP, half_width)).reshape(
        2 * EXPERTS, CAP, half_width
    )
    arrived = lax.all_to_all(outgoing, "wide", split_axis=0, concat_axis=1, tiled=True)
    inner_width = gate_up.shape[3]
    preact_local = jnp.einsum(
        "lrd,ldf->lrf",
        arrived,
        gate_up.reshape(local_halves, half_width, 2 * inner_width),
        preferred_element_type=F32,
    )
    rounded = round_keep(preact_local)
    summed = lax.psum(rounded.astype(BF16), "narrow").astype(F32)
    hidden = (jax.nn.silu(summed[:, :, :inner_width]) * summed[:, :, inner_width:]).astype(BF16)
    partial_out = jnp.einsum("lrf,lfd->lrd", hidden, expert_down, preferred_element_type=F32).astype(BF16)
    returned = lax.all_to_all(partial_out, "wide", split_axis=1, concat_axis=0, tiled=True)
    both_halves = returned.reshape(EXPERTS, 2, CAP, half_width).astype(F32)
    summed_rows = round_keep(both_halves[:, 0] + both_halves[:, 1]).reshape(EXPERTS * CAP, half_width)
    picked = summed_rows[target].reshape(token_count, TOP, half_width)
    mixed = jnp.sum(picked * route_gates[:, :, None], axis=1)
    return mixed.astype(BF16)


def ring_pairs(shift):
    return [(RING[i], RING[(i + shift) % NR]) for i in range(NR)]


def from_prev(value):
    return lax.ppermute(value, "wide", ring_pairs(1))


def from_next(value):
    return lax.ppermute(value, "wide", ring_pairs(-1))


def swap(value, axis):
    return lax.ppermute(value, axis, [(0, 1), (1, 0)])


def ring_gather(own, antipode_by_prev):
    got = [None] * NR
    got[0] = own
    for q in (1, 2, 3):
        got[q] = from_prev(got[q - 1])
        got[NR - q] = from_next(got[(NR - q + 1) % NR])
    got[4] = from_prev(got[3]) if antipode_by_prev else from_next(got[5])
    return got


def add(left, right):
    return (left.astype(F32) + right.astype(F32)).astype(BF16)


def ring_scatter(parts, antipode_by_next):
    if antipode_by_next:
        low = add(from_next(parts[4]), parts[3])
        high = parts[5]
    else:
        low = parts[3]
        high = add(from_prev(parts[4]), parts[5])
    for q in (2, 1, 0):
        low = from_next(low)
        high = from_prev(high)
        if q:
            low = add(low, parts[q])
            high = add(high, parts[NR - q])
    return (parts[0].astype(F32) + low.astype(F32) + high.astype(F32)).astype(BF16)


def prologue_kernel(
    experts,
    slots,
    tile_rows,
    *refs,
):
    n_tok = NR * slots
    meta, info = refs[0], refs[1]
    token_in = refs[2 : 2 + n_tok]
    weight_in = refs[2 + n_tok : 2 + n_tok + 2 * NR]
    rows_out, mix_out = refs[2 + n_tok + 2 * NR : 4 + n_tok + 2 * NR]
    tokens, weight, packed, token_sem, weight_sem = refs[4 + n_tok + 2 * NR :]
    part = weight_in[0].shape[0]
    copies = []
    for i, ref in enumerate(token_in):
        copies.append(pltpu.make_async_copy(ref, tokens.at[i], token_sem.at[i]))
    for i, ref in enumerate(weight_in):
        at = pl.multiple_of(meta[16 + i] * part, part)
        copies.append(pltpu.make_async_copy(ref, weight.at[pl.ds(at, part)], weight_sem.at[i]))
    for copy in copies:
        copy.start()

    first = meta[0].astype(F32)
    toks = slots * tile_rows
    before = lax.broadcasted_iota(jnp.int32, (toks, toks), 0) < lax.broadcasted_iota(jnp.int32, (toks, toks), 1)
    before = before.astype(F32).astype(BF16)
    ids = lax.broadcasted_iota(jnp.int32, (experts, toks), 0).astype(F32) + first
    place = lax.broadcasted_iota(jnp.int32, (experts, CAP, toks), 1).astype(F32)
    picks = []
    for q in range(NR):
        named = jnp.zeros((experts, toks), F32)
        gate = jnp.zeros((experts, toks), F32)
        for k in range(TOP):
            same = jnp.broadcast_to(info[q, k : k + 1, :], (experts, toks)) == ids
            named = jnp.where(same, 1.0, named)
            gate = jnp.where(same, jnp.broadcast_to(info[q, 8 + k : 9 + k, :], (experts, toks)), gate)
        rank = jnp.dot(named.astype(BF16), before, preferred_element_type=F32)
        rank = jnp.where(named > 0.0, rank, -1.0)
        chosen = jnp.broadcast_to(rank[:, None, :], (experts, CAP, toks)) == place
        pick = jnp.where(chosen, 1.0, 0.0).reshape(experts * CAP, toks)
        picks.append(pick.astype(BF16))
        gated = jnp.where(chosen, jnp.broadcast_to(gate[:, None, :], (experts, CAP, toks)), 0.0)
        gated = gated.reshape(experts * CAP, toks)
        coarse = gated.astype(BF16)
        mix_out[q, 0] = coarse
        mix_out[q, 1] = (gated - coarse.astype(F32)).astype(BF16)

    for copy in copies:
        copy.wait()

    missed = meta[1]
    most = packed.shape[0]
    for i in range(most):

        @pl.when(i < missed)
        def _(i=i):
            packed[i] = tokens[meta[2 + i]]

    for i in range(0, most, 2):

        @pl.when(i < missed)
        def _(i=i):
            rows = packed[i : i + 2].reshape(2 * tile_rows, packed.shape[2])
            coded = jnp.dot(rows, weight[...], preferred_element_type=F32).astype(BF16)
            tokens[meta[2 + i]] = coded[:tile_rows]

            @pl.when(i + 1 < missed)
            def _():
                tokens[meta[3 + i]] = coded[tile_rows:]

    for q in range(NR):
        source = tokens[q * slots : (q + 1) * slots].reshape(toks, tokens.shape[2])
        rows = jnp.dot(picks[q], source, preferred_element_type=F32).astype(BF16)
        rows_out[:, q * CAP : (q + 1) * CAP, :] = rows.reshape(experts, CAP, tokens.shape[2])


def first_kernel(base, count, rows, gate_up, out, wbuf, spread, sem):
    halves = 2 * count
    copies = [
        pltpu.make_async_copy(gate_up.at[2 * base + h], wbuf.at[h], sem.at[h]) for h in range(halves)
    ]
    for copy in copies:
        copy.start()
    width = rows.shape[2]
    most = rows.shape[1]
    inner = gate_up.shape[3]
    src = lax.broadcasted_iota(jnp.int32, (128, 256), 0)
    dst = lax.broadcasted_iota(jnp.int32, (128, 256), 1)
    even = (dst == 2 * src).astype(F32).astype(BF16)
    odd = (dst == 2 * src + 1).astype(F32).astype(BF16)
    for e in range(count):
        for c in range(width // 128):
            piece = rows[base + e, :, 128 * c : 128 * c + 128]
            spread[e, :most, 256 * c : 256 * c + 256] = jnp.dot(piece, even, preferred_element_type=F32).astype(BF16)
            spread[e, most:, 256 * c : 256 * c + 256] = jnp.dot(piece, odd, preferred_element_type=F32).astype(BF16)
    for h in range(halves):
        copies[h].wait()
        acc = jnp.dot(
            spread[h // 2], wbuf[h].reshape(2 * width, inner), preferred_element_type=F32
        )
        out[h, :, :inner] = acc[:most].astype(BF16)
        out[h, :, inner:] = acc[most:].astype(BF16)


def second_kernel(chunk, width, n_chunks, make_hidden, *refs):
    if make_hidden:
        own = refs[:n_chunks]
        other = refs[n_chunks : 2 * n_chunks]
        mix, down = refs[2 * n_chunks : 2 * n_chunks + 2]
        hidden = refs[2 * n_chunks + 2]
        outs = refs[2 * n_chunks + 3 : 2 * n_chunks + 3 + NR]
        wbuf, pairs, sem = refs[2 * n_chunks + 3 + NR :]
    else:
        hidden, mix, down = refs[:3]
        outs = refs[3 : 3 + NR]
        wbuf, pairs, sem = refs[3 + NR :]
    halves, _, inner = hidden.shape
    copies = [
        pltpu.make_async_copy(
            down.at[pl.ds(2 * e, 2), :, pl.ds(chunk * width, width)], wbuf.at[pl.ds(2 * e, 2)], sem.at[e]
        )
        for e in range(halves // 2)
    ]
    for copy in copies:
        copy.start()
    if make_hidden:
        per = halves // n_chunks
        for h in range(halves):
            pre = own[h // per][h % per].astype(F32) + other[h // per][h % per].astype(F32)
            gate, up = pre[:, :inner], pre[:, inner:]
            hidden[h] = (gate / (1.0 + jnp.exp(-gate)) * up).astype(BF16)
    for e in range(halves // 2):
        copies[e].wait()
        acc = jnp.dot(hidden[2 * e], wbuf[2 * e], preferred_element_type=F32)
        acc += jnp.dot(hidden[2 * e + 1], wbuf[2 * e + 1], preferred_element_type=F32)
        pairs[e] = acc.astype(BF16)
    dims = (((0,), (0,)), ((), ()))
    for q in range(NR):
        rows = pairs[:, q * CAP : (q + 1) * CAP, :].reshape(halves // 2 * CAP, width)
        total = lax.dot_general(mix[q, 0], rows, dims, preferred_element_type=F32)
        total += lax.dot_general(mix[q, 1], rows, dims, preferred_element_type=F32)
        outs[q][...] = total.astype(BF16)


def on_device_ring(
    tile_hidden, cached_rows, tile_image, cache_ids, adapter_weight, routes, route_gates, gate_up, expert_down
):
    slots, tile_rows, adapt_width = tile_hidden.shape
    toks = slots * tile_rows
    half_width = cached_rows.shape[1]
    halves, _, _, inner = gate_up.shape
    experts = halves // 2
    shard = adapter_weight.shape[0]
    part = shard // 2
    params = pltpu.CompilerParams(vmem_limit_bytes=VMEM_LIMIT)

    wide_id = lax.axis_index("wide")
    grp_id = lax.axis_index("grp")
    where_in_ring = [RING.index(w) for w in range(NR)]
    pos = jnp.asarray(where_in_ring, jnp.int32)[wide_id]
    sources = jnp.asarray(RING, jnp.int32)[(pos - jnp.arange(NR, dtype=jnp.int32)) % NR]

    weight_own = lax.dynamic_slice_in_dim(adapter_weight, grp_id * part, part, axis=0)
    weight_ring = ring_gather(weight_own, True)
    weight_other = [swap(value, "grp") for value in weight_ring]

    cache_hit = jnp.any(tile_image[:, None] == cache_ids[None, :], axis=1)
    sent = jnp.where(cache_hit[:, None, None], cached_rows.reshape(slots, tile_rows, half_width), activate(tile_hidden))
    info_own = jnp.concatenate(
        [
            routes.T.astype(F32),
            jnp.broadcast_to(jnp.where(cache_hit, 0.0, 1.0).astype(F32)[:, None], (slots, tile_rows)).reshape(1, toks),
            jnp.zeros((1, toks), F32),
            route_gates.T,
            jnp.zeros((2, toks), F32),
        ]
    )
    info = jnp.stack([info_own] + [lax.ppermute(info_own, "wide", ring_pairs(q)) for q in range(1, NR)])
    tokens = [ring_gather(sent[s], s % 2 == 0) for s in range(slots)]

    missed = info[:, 6, :].reshape(NR * slots, tile_rows)[:, 0] > 0.5
    rank = jnp.where(missed, jnp.cumsum(missed.astype(jnp.int32)) - 1, -1)
    most = NR * slots // 2
    at = jnp.arange(NR * slots, dtype=jnp.int32)
    missed_at = jnp.sum(
        jnp.where(rank[None, :] == jnp.arange(most, dtype=jnp.int32)[:, None], at[None, :], 0), axis=1
    )
    meta = jnp.concatenate(
        [
            (wide_id * experts).reshape(1).astype(jnp.int32),
            jnp.sum(missed.astype(jnp.int32)).reshape(1),
            missed_at.astype(jnp.int32),
            jnp.zeros((16 - 2 - most,), jnp.int32),
            sources * 2 + grp_id,
            sources * 2 + (1 - grp_id),
        ]
    )

    rows, mix = pl.pallas_call(
        functools.partial(prologue_kernel, experts, slots, tile_rows),
        in_specs=[SM, VM] + [ANY] * (NR * slots + 2 * NR),
        out_specs=[VM, VM],
        out_shape=[
            jax.ShapeDtypeStruct((experts, NR * CAP, half_width), BF16),
            jax.ShapeDtypeStruct((NR, 2, experts * CAP, toks), BF16),
        ],
        scratch_shapes=[
            pltpu.VMEM((NR * slots, tile_rows, half_width), BF16),
            pltpu.VMEM((NR * shard, half_width), BF16),
            pltpu.VMEM((most, tile_rows, half_width), BF16),
            pltpu.SemaphoreType.DMA((NR * slots,)),
            pltpu.SemaphoreType.DMA((2 * NR,)),
        ],
        compiler_params=params,
    )(meta, info, *[tokens[s][q] for q in range(NR) for s in range(slots)], *weight_ring, *weight_other)

    n_first = 4
    count = experts // n_first
    own, other = [], []
    for c in range(n_first):
        pre = pl.pallas_call(
            functools.partial(first_kernel, c * count, count),
            in_specs=[VM, ANY],
            out_specs=VM,
            out_shape=jax.ShapeDtypeStruct((2 * count, NR * CAP, 2 * inner), BF16),
            scratch_shapes=[
                pltpu.VMEM((2 * count, half_width, 2, inner), BF16),
                pltpu.VMEM((count, 2 * NR * CAP, 2 * half_width), BF16),
                pltpu.SemaphoreType.DMA((2 * count,)),
            ],
            compiler_params=params,
            cost_estimate=pl.CostEstimate(
                flops=4 * NR * CAP * half_width * 4 * count * inner,
                bytes_accessed=2 * count * half_width * 4 * inner,
                transcendentals=0,
            ),
        )(rows, gate_up)
        own.append(pre)
        other.append(swap(pre, "narrow"))

    n_second = 2
    width = half_width // n_second
    mixed = []
    hidden = None
    for c in range(n_second):
        part_shapes = [jax.ShapeDtypeStruct((toks, width), BF16)] * NR
        scratch = [
            pltpu.VMEM((halves, inner, width), BF16),
            pltpu.VMEM((experts, NR * CAP, width), BF16),
            pltpu.SemaphoreType.DMA((experts,)),
        ]
        cost = pl.CostEstimate(
            flops=2 * halves * NR * CAP * inner * width,
            bytes_accessed=2 * halves * inner * width,
            transcendentals=0,
        )
        if hidden is None:
            hidden, *parts = pl.pallas_call(
                functools.partial(second_kernel, c, width, n_first, True),
                in_specs=[VM] * (2 * n_first) + [VM, ANY],
                out_specs=[VM] * (NR + 1),
                out_shape=[jax.ShapeDtypeStruct((halves, NR * CAP, inner), BF16)] + part_shapes,
                scratch_shapes=scratch,
                compiler_params=params,
                cost_estimate=cost,
            )(*own, *other, mix, expert_down)
        else:
            parts = pl.pallas_call(
                functools.partial(second_kernel, c, width, n_first, False),
                in_specs=[VM, VM, ANY],
                out_specs=[VM] * NR,
                out_shape=part_shapes,
                scratch_shapes=scratch,
                compiler_params=params,
                cost_estimate=cost,
            )(hidden, mix, expert_down)
        mixed.append(ring_scatter(parts, c % 2 == 0))
    return jnp.concatenate(mixed, axis=1)


def solution(mesh):
    body = on_device_ring if mesh.shape["wide"] == NR else on_device_plain
    return jax.shard_map(
        body,
        mesh=mesh,
        in_specs=(
            P(("grp", "wide"), None, None),
            P(("grp", "wide"), "narrow"),
            P(("grp", "wide")),
            P("grp"),
            P("wide", "narrow"),
            P(("grp", "wide"), None),
            P(("grp", "wide"), None),
            P("wide", "narrow", None, None),
            P("wide", None, "narrow"),
        ),
        out_specs=P(("grp", "wide"), "narrow"),
        check_vma=False,
    )
```

```python
import functools
import math

import jax
import jax.numpy as jnp
from jax import lax
from jax.experimental import pallas as pl
from jax.experimental.pallas import tpu as pltpu
from jax.sharding import PartitionSpec as P

EXPERTS = 64
TOP = 6
CAP = 16
F32 = jnp.float32
BF16 = jnp.bfloat16
RING = (0, 2, 4, 6, 7, 5, 3, 1)
NR = 8
VMEM_LIMIT = 46 << 20
VMEM_SMALL = 14 << 20
FETCH_LIMITS = (40, 33, 24, 16)
ANY = pl.BlockSpec(memory_space=pl.ANY)
VM = pl.BlockSpec(memory_space=pltpu.VMEM)


def activate(tiles):
    return jax.nn.gelu(tiles.astype(F32), approximate=False).astype(BF16)


def round_keep(values):
    return lax.optimization_barrier(values.astype(BF16)).astype(F32)


def on_device_plain(
    tile_hidden, cached_rows, tile_image, cache_ids, adapter_weight, routes, route_gates, gate_up, expert_down
):
    slot_count, tile_rows, adapt_width = tile_hidden.shape
    half_width = cached_rows.shape[1]
    cache_hit = jnp.any(tile_image[:, None] == cache_ids[None, :], axis=1)
    whole_weight = lax.all_gather(adapter_weight, "wide", axis=0, tiled=True)
    active = activate(tile_hidden).reshape(slot_count * tile_rows, adapt_width)
    encoded = jnp.dot(active, whole_weight, preferred_element_type=F32).astype(BF16)
    token_count = slot_count * tile_rows
    hit_rows = jnp.repeat(cache_hit, tile_rows)
    tokens_in = jnp.where(hit_rows[:, None], cached_rows, encoded)
    expert_flat = routes.reshape(-1)
    pair_count = expert_flat.shape[0]
    onehot = (expert_flat[:, None] == jnp.arange(EXPERTS, dtype=jnp.int32)[None, :]).astype(jnp.int32)
    earlier = jnp.cumsum(onehot, axis=0) - onehot
    slot_index = jnp.sum(earlier * onehot, axis=1)
    target = expert_flat * CAP + slot_index
    owner_table = (
        jnp.full((EXPERTS * CAP,), token_count, jnp.int32)
        .at[target]
        .set(jnp.arange(pair_count, dtype=jnp.int32) // TOP)
    )
    padded_tokens = jnp.concatenate([tokens_in, jnp.zeros((1, half_width), BF16)])
    expert_rows = padded_tokens[owner_table].reshape(EXPERTS, CAP, half_width)
    local_halves = gate_up.shape[0]
    outgoing = jnp.broadcast_to(expert_rows[:, None], (EXPERTS, 2, CAP, half_width)).reshape(
        2 * EXPERTS, CAP, half_width
    )
    arrived = lax.all_to_all(outgoing, "wide", split_axis=0, concat_axis=1, tiled=True)
    inner_width = gate_up.shape[3]
    preact_local = jnp.einsum(
        "lrd,ldf->lrf",
        arrived,
        gate_up.reshape(local_halves, half_width, 2 * inner_width),
        preferred_element_type=F32,
    )
    rounded = round_keep(preact_local)
    summed = lax.psum(rounded.astype(BF16), "narrow").astype(F32)
    hidden = (jax.nn.silu(summed[:, :, :inner_width]) * summed[:, :, inner_width:]).astype(BF16)
    partial_out = jnp.einsum("lrf,lfd->lrd", hidden, expert_down, preferred_element_type=F32).astype(BF16)
    returned = lax.all_to_all(partial_out, "wide", split_axis=1, concat_axis=0, tiled=True)
    both_halves = returned.reshape(EXPERTS, 2, CAP, half_width).astype(F32)
    summed_rows = round_keep(both_halves[:, 0] + both_halves[:, 1]).reshape(EXPERTS * CAP, half_width)
    picked = summed_rows[target].reshape(token_count, TOP, half_width)
    mixed = jnp.sum(picked * route_gates[:, :, None], axis=1)
    return mixed.astype(BF16)


def ring_pairs(shift):
    return [(RING[i], RING[(i + shift) % NR]) for i in range(NR)]


def from_prev(value):
    return lax.ppermute(value, "wide", ring_pairs(1))


def from_next(value):
    return lax.ppermute(value, "wide", ring_pairs(-1))


def swap(value, axis):
    return lax.ppermute(value, axis, [(0, 1), (1, 0)])


def tie(*values):
    return lax.optimization_barrier(values)


def ring_gather_two(first, make_second, fetches):
    one, two = [first] * NR, [None] * NR
    fetched = []
    far = NR // 2
    for q in range(1, far + 1):
        up, down = one[q - 1], one[(NR - q + 1) % NR]
        if q > 2:
            up, down, two[q - 2], two[NR - q + 2] = tie(up, down, two[q - 2], two[NR - q + 2])
        if q < far:
            one[q], one[NR - q] = from_prev(up), from_next(down)
        else:
            one[q] = from_next(down)
        if q == 1:
            two[0], one[1], one[NR - 1] = make_second(one[1], one[NR - 1])
        up, down = two[q - 1], two[(NR - q + 1) % NR]
        if q > 1:
            up, down, one[q], one[NR - q], *fetched = tie(up, down, one[q], one[NR - q], *fetched)
        if q < far:
            two[q], two[NR - q] = from_prev(up), from_next(down)
            if fetches:
                fetched.append(fetches.pop(0)())
        else:
            two[q] = from_prev(up)
            fetched += [make() for make in fetches]
    return one, two, fetched


def add(left, right):
    return (left.astype(F32) + right.astype(F32)).astype(BF16)


def ring_scatter(parts, antipode_by_next):
    if antipode_by_next:
        low = add(from_next(parts[4]), parts[3])
        high = parts[5]
    else:
        low = parts[3]
        high = add(from_prev(parts[4]), parts[5])
    for q in (2, 1, 0):
        low = from_next(low)
        high = from_prev(high)
        if q:
            low = add(low, parts[q])
            high = add(high, parts[NR - q])
    return (parts[0].astype(F32) + low.astype(F32) + high.astype(F32)).astype(BF16)


def ring_source(q):
    wide_id = lax.axis_index("wide")
    level = wide_id // 2
    pos = jnp.where(wide_id % 2 == 1, NR - 1 - level, level)
    pos = (pos + NR - q) % NR
    return jnp.where(pos < NR // 2, 2 * pos, 2 * (NR - 1 - pos) + 1)


def prologue_kernel(experts, slots, tile_rows, *refs):
    toks = slots * tile_rows
    sent_in, weight_in, gate_up = refs[:NR], refs[NR : 2 * NR], refs[2 * NR : -11]
    rows_out, mix_out, pre_out, sent, weight, packed, rows_here, missed_at, sent_sem, weight_sem = refs[-10:]
    near = rows_here.shape[0]
    shard = weight_in[0].shape[0]
    width = packed.shape[2]
    sent_copies = [pltpu.make_async_copy(ref, sent.at[q], sent_sem.at[q]) for q, ref in enumerate(sent_in)]
    copies = []
    for q, ref in enumerate(weight_in):
        at = pl.multiple_of(ring_source(q) * shard, shard)
        copies.append(pltpu.make_async_copy(ref, weight.at[pl.ds(at, shard)], weight_sem.at[q]))
    for copy in sent_copies + copies:
        copy.start()

    first = (lax.axis_index("wide") * experts).astype(F32)
    before = lax.broadcasted_iota(jnp.int32, (toks, toks), 0) < lax.broadcasted_iota(jnp.int32, (toks, toks), 1)
    before = before.astype(F32).astype(BF16)
    ids = lax.broadcasted_iota(jnp.int32, (experts, toks), 0).astype(F32) + first
    place = lax.broadcasted_iota(jnp.int32, (experts, CAP, toks), 1).astype(F32)
    picks = []
    missed = jnp.int32(0)
    for q in range(NR):
        sent_copies[q].wait()
        info = sent[q, toks:].astype(F32)
        for s in range(slots):
            flag = info[TOP + s, 0] > 0.5
            missed_at[missed] = q * slots + s
            missed = missed + flag.astype(jnp.int32)
        named = jnp.zeros((experts, toks), F32)
        gate = jnp.zeros((experts, toks), F32)
        for k in range(TOP):
            same = jnp.broadcast_to(info[k : k + 1, :toks], (experts, toks)) == ids
            named = jnp.where(same, 1.0, named)
            value = info[k : k + 1, toks : 2 * toks] + info[k : k + 1, 2 * toks : 3 * toks]
            value = value + info[k : k + 1, 3 * toks : 4 * toks]
            gate = jnp.where(same, jnp.broadcast_to(value, (experts, toks)), gate)
        rank = jnp.dot(named.astype(BF16), before, preferred_element_type=F32)
        rank = jnp.where(named > 0.0, rank, -1.0)
        chosen = jnp.broadcast_to(rank[:, None, :], (experts, CAP, toks)) == place
        pick = jnp.where(chosen, 1.0, 0.0).reshape(experts * CAP, toks)
        picks.append(pick.astype(BF16))
        gated = jnp.where(chosen, jnp.broadcast_to(gate[:, None, :], (experts, CAP, toks)), 0.0)
        gated = gated.reshape(experts * CAP, toks)
        coarse = gated.astype(BF16)
        mix_out[q, 0] = coarse
        mix_out[q, 1] = (gated - coarse.astype(F32)).astype(BF16)

    most = packed.shape[0]

    def tile_of(i):
        n = missed_at[i]
        return sent.at[n // slots, pl.ds(pl.multiple_of((n % slots) * tile_rows, tile_rows), tile_rows)]

    for i in range(most):

        @pl.when(i < missed)
        def _(i=i):
            packed[i] = tile_of(i)[...]

    for copy in copies:
        copy.wait()

    group = 4
    for i in range(0, most, group):

        @pl.when(i < missed)
        def _(i=i):
            rows = packed[i : i + group].reshape(group * tile_rows, width)
            coded = jnp.dot(rows, weight[...], preferred_element_type=F32).astype(BF16)
            for j in range(group):

                @pl.when(i + j < missed)
                def _(j=j):
                    tile_of(i + j)[...] = coded[j * tile_rows : (j + 1) * tile_rows]

    for q in range(NR):
        rows = jnp.dot(picks[q], sent[q, :toks], preferred_element_type=F32).astype(BF16)
        rows = rows.reshape(experts, CAP, width)
        rows_here[:, q * CAP : (q + 1) * CAP, :] = rows[:near]
        rows_out[:, q * CAP : (q + 1) * CAP, :] = rows[near:]
    first_matmuls(rows_here, gate_up, pre_out)


def first_matmuls(rows, weights, out):
    per = weights[0].shape[0]
    for h in range(out.shape[0]):
        out[h] = jnp.dot(rows[h // 2], weights[h // per][h % per], preferred_element_type=F32).astype(BF16)


def fetch_kernel(base, gate_up, out, buf, sem):
    halves, width, _ = out.shape
    inner = gate_up.shape[3]
    copies = [pltpu.make_async_copy(gate_up.at[base + h], buf.at[h], sem.at[h]) for h in range(halves)]
    for copy in copies:
        copy.start()
    rows = 128
    dst = lax.broadcasted_iota(jnp.int32, (2 * rows, 2 * rows), 0)
    src = lax.broadcasted_iota(jnp.int32, (2 * rows, 2 * rows), 1)
    parting = (src == jnp.where(dst < rows, 2 * dst, 2 * (dst - rows) + 1)).astype(F32).astype(BF16)
    for h in range(halves):
        copies[h].wait()
        for k in range(0, width, rows):
            mixed = buf[h, k : k + rows].reshape(2 * rows, inner)
            parted = jnp.dot(parting, mixed, preferred_element_type=F32).astype(BF16)
            out[h, k : k + rows, :inner] = parted[:rows]
            out[h, k : k + rows, inner:] = parted[rows:]


def first_kernel(rows, *refs):
    first_matmuls(rows, refs[:-1], refs[-1])


def gated_hidden(own, other):
    pre = own.astype(F32) + other.astype(F32)
    inner = pre.shape[1] // 2
    gate, up = pre[:, :inner], pre[:, inner:]
    return (gate / (1.0 + jnp.exp(-gate)) * up).astype(BF16)


def second_near_kernel(own, other, down, pairs, wbuf, sem):
    experts = pairs.shape[0]
    copies = [
        pltpu.make_async_copy(down.at[pl.ds(2 * e, 2)], wbuf.at[pl.ds(2 * e, 2)], sem.at[e]) for e in range(experts)
    ]
    for copy in copies:
        copy.start()
    for e in range(experts):
        hidden = [gated_hidden(own[h], other[h]) for h in (2 * e, 2 * e + 1)]
        copies[e].wait()
        acc = jnp.dot(hidden[0], wbuf[2 * e], preferred_element_type=F32)
        acc += jnp.dot(hidden[1], wbuf[2 * e + 1], preferred_element_type=F32)
        pairs[e] = acc.astype(BF16)


def second_far_kernel(base, chunk, width, *refs):
    if len(refs) == 5 + NR + 4:
        own, other, near_pairs, mix, down, hidden = refs[:6]
        outs = refs[6 : 6 + NR]
    else:
        hidden, near_pairs, mix, down = refs[:4]
        outs = refs[4 : 4 + NR]
        own = None
    pairs, wbuf, sem = refs[-3:]
    experts = pairs.shape[0]
    at = chunk * width
    copies = [
        pltpu.make_async_copy(
            down.at[pl.ds(base + 2 * e, 2), :, pl.ds(at, width)], wbuf.at[pl.ds(2 * e, 2)], sem.at[e]
        )
        for e in range(experts)
    ]
    for copy in copies:
        copy.start()
    if own is not None:
        for h in range(2 * experts):
            hidden[h] = gated_hidden(own[h], other[h])
    for e in range(experts):
        copies[e].wait()
        acc = jnp.dot(hidden[2 * e], wbuf[2 * e], preferred_element_type=F32)
        acc += jnp.dot(hidden[2 * e + 1], wbuf[2 * e + 1], preferred_element_type=F32)
        pairs[e] = acc.astype(BF16)
    dims = (((0,), (0,)), ((), ()))
    near = near_pairs.shape[0]
    for q in range(NR):
        span = slice(q * CAP, (q + 1) * CAP)
        rows = jnp.concatenate([near_pairs[:, span, at : at + width], pairs[:, span, :]], axis=0)
        rows = rows.reshape((near + experts) * CAP, width)
        total = lax.dot_general(mix[q, 0], rows, dims, preferred_element_type=F32)
        total += lax.dot_general(mix[q, 1], rows, dims, preferred_element_type=F32)
        outs[q][...] = total.astype(BF16)


def split3(values):
    high = values.astype(BF16)
    rest = values - high.astype(F32)
    middle = rest.astype(BF16)
    return high, middle, (rest - middle.astype(F32)).astype(BF16)


def on_device_ring(
    tile_hidden, cached_rows, tile_image, cache_ids, adapter_weight, routes, route_gates, gate_up, expert_down
):
    slots, tile_rows, adapt_width = tile_hidden.shape
    toks = slots * tile_rows
    half_width = cached_rows.shape[1]
    halves, _, _, inner = gate_up.shape
    experts = halves // 2
    shard = adapter_weight.shape[0]
    params = pltpu.CompilerParams(vmem_limit_bytes=VMEM_LIMIT)

    def message(*passing):
        hidden, *passing = tie(tile_hidden, *passing)
        cache_hit = jnp.any(tile_image[:, None] == cache_ids[None, :], axis=1)
        tokens_own = jnp.where(
            cache_hit[:, None, None], cached_rows.reshape(slots, tile_rows, half_width), activate(hidden)
        ).reshape(toks, half_width)
        flags = jnp.broadcast_to(jnp.where(cache_hit, 0.0, 1.0).astype(BF16)[:, None], (slots, toks))
        info_own = jnp.concatenate([routes.T.astype(BF16), flags, jnp.zeros((16 - TOP - slots, toks), BF16)])
        gates = [jnp.pad(piece, ((0, 16 - TOP), (0, 0))) for piece in split3(route_gates.T)]
        info_own = jnp.concatenate([info_own] + gates, axis=1)
        info_own = jnp.pad(info_own, ((0, 0), (0, half_width - 4 * toks)))
        return jnp.concatenate([tokens_own, info_own]), *passing

    def fetch(base, count, limit):
        shape = (count, half_width, 2 * inner)
        return pl.pallas_call(
            functools.partial(fetch_kernel, base),
            in_specs=[ANY],
            out_specs=VM,
            out_shape=jax.ShapeDtypeStruct(shape, BF16),
            scratch_shapes=[
                pltpu.VMEM((count, half_width, 2, inner), BF16),
                pltpu.SemaphoreType.DMA((count,)),
            ],
            compiler_params=pltpu.CompilerParams(vmem_limit_bytes=limit << 20),
            cost_estimate=pl.CostEstimate(
                flops=512 * count * half_width * 2 * inner, bytes_accessed=8 * count * half_width * inner, transcendentals=0
            ),
        )(gate_up)

    near = experts // 2
    far = experts - near
    count = halves // len(FETCH_LIMITS)
    fetches = [functools.partial(fetch, i * count, count, limit) for i, limit in enumerate(FETCH_LIMITS)]
    weight_ring, sent, fetched = ring_gather_two(adapter_weight, message, fetches)
    fetched_near, fetched_far = fetched[: len(fetched) // 2], fetched[len(fetched) // 2 :]
    most = NR * CAP
    pre_shape = jax.ShapeDtypeStruct((2 * near, most, 2 * inner), BF16)
    rows, mix, own_near = pl.pallas_call(
        functools.partial(prologue_kernel, experts, slots, tile_rows),
        in_specs=[ANY] * (2 * NR) + [VM] * len(fetched_near) + [ANY],
        out_specs=[VM, VM, VM],
        out_shape=[
            jax.ShapeDtypeStruct((far, most, half_width), BF16),
            jax.ShapeDtypeStruct((NR, 2, experts * CAP, toks), BF16),
            pre_shape,
        ],
        scratch_shapes=[
            pltpu.VMEM((NR, toks + 16, half_width), BF16),
            pltpu.VMEM((NR * shard, half_width), BF16),
            pltpu.VMEM((NR * slots // 2, tile_rows, half_width), BF16),
            pltpu.VMEM((near, most, half_width), BF16),
            pltpu.SMEM((NR * slots,), jnp.int32),
            pltpu.SemaphoreType.DMA((NR,)),
            pltpu.SemaphoreType.DMA((NR,)),
        ],
        compiler_params=pltpu.CompilerParams(vmem_limit_bytes=VMEM_SMALL),
    )(*sent, *weight_ring, *fetched_near, fetched_far[-1])
    other_near = swap(own_near, "narrow")

    own_far = pl.pallas_call(
        first_kernel,
        in_specs=[VM] * (1 + len(fetched_far)),
        out_specs=VM,
        out_shape=jax.ShapeDtypeStruct((2 * far, most, 2 * inner), BF16),
        compiler_params=pltpu.CompilerParams(vmem_limit_bytes=VMEM_SMALL),
        cost_estimate=pl.CostEstimate(
            flops=16 * most * half_width * far * inner, bytes_accessed=8 * far * half_width * inner, transcendentals=0
        ),
    )(rows, *fetched_far)
    own_far, other_near = tie(own_far, other_near)
    other_far = swap(own_far, "narrow")

    near_pairs = pl.pallas_call(
        second_near_kernel,
        in_specs=[VM, VM, ANY],
        out_specs=VM,
        out_shape=jax.ShapeDtypeStruct((near, most, half_width), BF16),
        scratch_shapes=[pltpu.VMEM((2 * near, inner, half_width), BF16), pltpu.SemaphoreType.DMA((near,))],
        compiler_params=params,
        cost_estimate=pl.CostEstimate(
            flops=4 * near * most * inner * half_width,
            bytes_accessed=4 * near * inner * half_width,
            transcendentals=2 * near * most * inner,
        ),
    )(own_near, other_near, expert_down)
    near_pairs, other_far = tie(near_pairs, other_far)

    n_second = 2
    width = half_width // n_second
    mixed = []
    hidden = None
    for c in range(n_second):
        start = hidden is None
        out = pl.pallas_call(
            functools.partial(second_far_kernel, 2 * near, c, width),
            in_specs=[VM] * (4 if start else 3) + [ANY],
            out_specs=[VM] * (start + NR),
            out_shape=[jax.ShapeDtypeStruct((2 * far, most, inner), BF16)] * start
            + [jax.ShapeDtypeStruct((toks, width), BF16)] * NR,
            scratch_shapes=[
                pltpu.VMEM((far, most, width), BF16),
                pltpu.VMEM((2 * far, inner, width), BF16),
                pltpu.SemaphoreType.DMA((far,)),
            ],
            compiler_params=params,
            cost_estimate=pl.CostEstimate(
                flops=4 * far * most * inner * width, bytes_accessed=4 * far * inner * width, transcendentals=0
            ),
        )(*((own_far, other_far) if start else (hidden,)), near_pairs, mix, expert_down)
        if start:
            hidden, *out = out
        mixed.append(ring_scatter(out, c % 2 == 0))
    return jnp.concatenate(mixed, axis=1)


def solution(mesh):
    body = on_device_ring if mesh.shape["wide"] == NR else on_device_plain
    return jax.shard_map(
        body,
        mesh=mesh,
        in_specs=(
            P(("grp", "wide"), None, None),
            P(("grp", "wide"), "narrow"),
            P(("grp", "wide")),
            P("grp"),
            P("wide", "narrow"),
            P(("grp", "wide"), None),
            P(("grp", "wide"), None),
            P("wide", "narrow", None, None),
            P("wide", None, "narrow"),
        ),
        out_specs=P(("grp", "wide"), "narrow"),
        check_vma=False,
    )
```

```python
import functools
import math

import jax
import jax.numpy as jnp
from jax import lax
from jax.experimental import pallas as pl
from jax.experimental.pallas import tpu as pltpu
from jax.sharding import PartitionSpec as P

EXPERTS = 64
TOP = 6
CAP = 16
F32 = jnp.float32
BF16 = jnp.bfloat16
RING = (0, 2, 4, 6, 7, 5, 3, 1)
NR = 8
CROSSING = ((1, 7, 2, 6), (3, 5), (4,))
VMEM_LIMIT = 46 << 20
VMEM_SMALL = 10 << 20
VMEM_FAR = 25 << 20
FETCH_LIMITS = (34, 26, 18)
ANY = pl.BlockSpec(memory_space=pl.ANY)
VM = pl.BlockSpec(memory_space=pltpu.VMEM)


def activate(tiles):
    return jax.nn.gelu(tiles.astype(F32), approximate=False).astype(BF16)


def round_keep(values):
    return lax.optimization_barrier(values.astype(BF16)).astype(F32)


def on_device_plain(
    tile_hidden, cached_rows, tile_image, cache_ids, adapter_weight, routes, route_gates, gate_up, expert_down
):
    slot_count, tile_rows, adapt_width = tile_hidden.shape
    half_width = cached_rows.shape[1]
    cache_hit = jnp.any(tile_image[:, None] == cache_ids[None, :], axis=1)
    whole_weight = lax.all_gather(adapter_weight, "wide", axis=0, tiled=True)
    active = activate(tile_hidden).reshape(slot_count * tile_rows, adapt_width)
    encoded = jnp.dot(active, whole_weight, preferred_element_type=F32).astype(BF16)
    token_count = slot_count * tile_rows
    hit_rows = jnp.repeat(cache_hit, tile_rows)
    tokens_in = jnp.where(hit_rows[:, None], cached_rows, encoded)
    expert_flat = routes.reshape(-1)
    pair_count = expert_flat.shape[0]
    onehot = (expert_flat[:, None] == jnp.arange(EXPERTS, dtype=jnp.int32)[None, :]).astype(jnp.int32)
    earlier = jnp.cumsum(onehot, axis=0) - onehot
    slot_index = jnp.sum(earlier * onehot, axis=1)
    target = expert_flat * CAP + slot_index
    owner_table = (
        jnp.full((EXPERTS * CAP,), token_count, jnp.int32)
        .at[target]
        .set(jnp.arange(pair_count, dtype=jnp.int32) // TOP)
    )
    padded_tokens = jnp.concatenate([tokens_in, jnp.zeros((1, half_width), BF16)])
    expert_rows = padded_tokens[owner_table].reshape(EXPERTS, CAP, half_width)
    local_halves = gate_up.shape[0]
    outgoing = jnp.broadcast_to(expert_rows[:, None], (EXPERTS, 2, CAP, half_width)).reshape(
        2 * EXPERTS, CAP, half_width
    )
    arrived = lax.all_to_all(outgoing, "wide", split_axis=0, concat_axis=1, tiled=True)
    inner_width = gate_up.shape[3]
    preact_local = jnp.einsum(
        "lrd,ldf->lrf",
        arrived,
        gate_up.reshape(local_halves, half_width, 2 * inner_width),
        preferred_element_type=F32,
    )
    rounded = round_keep(preact_local)
    summed = lax.psum(rounded.astype(BF16), "narrow").astype(F32)
    hidden = (jax.nn.silu(summed[:, :, :inner_width]) * summed[:, :, inner_width:]).astype(BF16)
    partial_out = jnp.einsum("lrf,lfd->lrd", hidden, expert_down, preferred_element_type=F32).astype(BF16)
    returned = lax.all_to_all(partial_out, "wide", split_axis=1, concat_axis=0, tiled=True)
    both_halves = returned.reshape(EXPERTS, 2, CAP, half_width).astype(F32)
    summed_rows = round_keep(both_halves[:, 0] + both_halves[:, 1]).reshape(EXPERTS * CAP, half_width)
    picked = summed_rows[target].reshape(token_count, TOP, half_width)
    mixed = jnp.sum(picked * route_gates[:, :, None], axis=1)
    return mixed.astype(BF16)


def ring_pairs(shift):
    return [(RING[i], RING[(i + shift) % NR]) for i in range(NR)]


def from_prev(value):
    return lax.ppermute(value, "wide", ring_pairs(1))


def from_next(value):
    return lax.ppermute(value, "wide", ring_pairs(-1))


def swap(value, axis):
    return lax.ppermute(value, axis, [(0, 1), (1, 0)])


def tie(*values):
    return lax.optimization_barrier(values)


def ring_gather_two(first, make_second, fetches):
    one, two = [first] * NR, [None] * NR
    fetched, across = [], []
    far = NR // 2
    for q in range(1, far + 1):
        up, down = one[q - 1], one[(NR - q + 1) % NR]
        if q > 2:
            up, down, two[q - 2], two[NR - q + 2] = tie(up, down, two[q - 2], two[NR - q + 2])
        if q < far:
            one[q], one[NR - q] = from_prev(up), from_next(down)
        else:
            one[q] = from_next(down)
        if q == 1:
            two[0], one[1], one[NR - 1] = tie(make_second(), one[1], one[NR - 1])
        up, down = two[q - 1], two[(NR - q + 1) % NR]
        if 1 < q < far:
            up, down, one[q], one[NR - q], *fetched = tie(up, down, one[q], one[NR - q], *fetched)
        elif q == far:
            up, two[NR - q + 1], one[q], across[0], *fetched = tie(up, two[NR - q + 1], one[q], across[0], *fetched)
        if q < far:
            two[q], two[NR - q] = from_prev(up), from_next(down)
            if fetches:
                fetched.append(fetches.pop(0)())
        else:
            two[q] = from_prev(up)
        if q == far // 2:
            across.append(swap(jnp.concatenate([one[p] for p in CROSSING[0]]), "grp"))
        elif q > far // 2:
            pieces = [one[p] for p in CROSSING[q - far // 2]]
            across.append(swap(jnp.concatenate(pieces) if len(pieces) > 1 else pieces[0], "grp"))
    return one, two, fetched, across


def add(left, right):
    return (left.astype(F32) + right.astype(F32)).astype(BF16)


def ring_scatter(parts, antipode_by_next):
    if antipode_by_next:
        low = add(from_next(parts[4]), parts[3])
        high = parts[5]
    else:
        low = parts[3]
        high = add(from_prev(parts[4]), parts[5])
    for q in (2, 1, 0):
        low = from_next(low)
        high = from_prev(high)
        if q:
            low = add(low, parts[q])
            high = add(high, parts[NR - q])
    return (parts[0].astype(F32) + low.astype(F32) + high.astype(F32)).astype(BF16)


def ring_source(q):
    wide_id = lax.axis_index("wide")
    level = wide_id // 2
    pos = jnp.where(wide_id % 2 == 1, NR - 1 - level, level)
    pos = (pos + NR - q) % NR
    return jnp.where(pos < NR // 2, 2 * pos, 2 * (NR - 1 - pos) + 1)


def prologue_kernel(experts, slots, tile_rows, *refs):
    toks = slots * tile_rows
    sent_in = refs[:NR]
    weight_own, weight_ring = refs[NR], refs[NR + 1 : 2 * NR]
    weight_across = refs[2 * NR : 2 * NR + len(CROSSING)]
    gate_up = refs[2 * NR + len(CROSSING) : -8]
    rows_out, mix_out, pre_out, sent, weight, packed, rows_here, missed_at = refs[-8:]
    near = rows_here.shape[0]
    shard = weight_own.shape[0]
    part = shard // 2
    width = packed.shape[2]
    grp_id = lax.axis_index("grp")
    pieces = [(weight_own, 0, 0, shard)]
    for q in range(1, NR):
        pieces.append((weight_ring[q - 1], q, grp_id * part, part))
    for batch, group in zip(weight_across, CROSSING):
        for i, q in enumerate(group):
            pieces.append((batch.at[pl.ds(i * part, part)], q, (1 - grp_id) * part, part))
    for q, ref in enumerate(sent_in):
        sent[q] = ref[...]
    for ref, q, begin, count in pieces:
        at = pl.multiple_of(ring_source(q) * shard + begin, part)
        weight[pl.ds(at, count)] = ref[...]

    first = (lax.axis_index("wide") * experts).astype(F32)
    before = lax.broadcasted_iota(jnp.int32, (toks, toks), 0) < lax.broadcasted_iota(jnp.int32, (toks, toks), 1)
    before = before.astype(F32).astype(BF16)
    ids = lax.broadcasted_iota(jnp.int32, (experts, toks), 0).astype(F32) + first
    place = lax.broadcasted_iota(jnp.int32, (experts, CAP, toks), 1).astype(F32)
    picks = []
    missed = jnp.int32(0)
    for q in range(NR):
        info = sent[q, toks:].astype(F32)
        for s in range(slots):
            flag = info[TOP + s, 0] > 0.5
            missed_at[missed] = q * slots + s
            missed = missed + flag.astype(jnp.int32)
        named = jnp.zeros((experts, toks), F32)
        gate = jnp.zeros((experts, toks), F32)
        for k in range(TOP):
            same = jnp.broadcast_to(info[k : k + 1, :toks], (experts, toks)) == ids
            named = jnp.where(same, 1.0, named)
            value = info[k : k + 1, toks : 2 * toks] + info[k : k + 1, 2 * toks : 3 * toks]
            value = value + info[k : k + 1, 3 * toks : 4 * toks]
            gate = jnp.where(same, jnp.broadcast_to(value, (experts, toks)), gate)
        rank = jnp.dot(named.astype(BF16), before, preferred_element_type=F32)
        rank = jnp.where(named > 0.0, rank, -1.0)
        chosen = jnp.broadcast_to(rank[:, None, :], (experts, CAP, toks)) == place
        pick = jnp.where(chosen, 1.0, 0.0).reshape(experts * CAP, toks)
        picks.append(pick.astype(BF16))
        gated = jnp.where(chosen, jnp.broadcast_to(gate[:, None, :], (experts, CAP, toks)), 0.0)
        gated = gated.reshape(experts * CAP, toks)
        coarse = gated.astype(BF16)
        mix_out[q, 0] = coarse
        mix_out[q, 1] = (gated - coarse.astype(F32)).astype(BF16)

    most = packed.shape[0]

    def tile_of(i):
        n = missed_at[i]
        return sent.at[n // slots, pl.ds(pl.multiple_of((n % slots) * tile_rows, tile_rows), tile_rows)]

    for i in range(most):

        @pl.when(i < missed)
        def _(i=i):
            packed[i] = tile_of(i)[...]

    group = 4
    for i in range(0, most, group):

        @pl.when(i < missed)
        def _(i=i):
            rows = packed[i : i + group].reshape(group * tile_rows, width)
            coded = jnp.dot(rows, weight[...], preferred_element_type=F32).astype(BF16)
            for j in range(group):

                @pl.when(i + j < missed)
                def _(j=j):
                    tile_of(i + j)[...] = coded[j * tile_rows : (j + 1) * tile_rows]

    for q in range(NR):
        rows = jnp.dot(picks[q], sent[q, :toks], preferred_element_type=F32).astype(BF16)
        rows = rows.reshape(experts, CAP, width)
        rows_here[:, q * CAP : (q + 1) * CAP, :] = rows[:near]
        rows_out[:, q * CAP : (q + 1) * CAP, :] = rows[near:]
    first_matmuls(rows_here, gate_up, pre_out)


def first_matmuls(rows, weights, out):
    per = weights[0].shape[0]
    for h in range(out.shape[0]):
        out[h] = jnp.dot(rows[h // 2], weights[h // per][h % per], preferred_element_type=F32).astype(BF16)


def fetch_kernel(base, gate_up, out, buf, sem):
    halves, width, _ = out.shape
    inner = gate_up.shape[3]
    copies = [pltpu.make_async_copy(gate_up.at[base + h], buf.at[h], sem.at[h]) for h in range(halves)]
    for copy in copies:
        copy.start()
    rows = 128
    dst = lax.broadcasted_iota(jnp.int32, (2 * rows, 2 * rows), 0)
    src = lax.broadcasted_iota(jnp.int32, (2 * rows, 2 * rows), 1)
    parting = (src == jnp.where(dst < rows, 2 * dst, 2 * (dst - rows) + 1)).astype(F32).astype(BF16)
    for h in range(halves):
        copies[h].wait()
        for k in range(0, width, rows):
            mixed = buf[h, k : k + rows].reshape(2 * rows, inner)
            parted = jnp.dot(parting, mixed, preferred_element_type=F32).astype(BF16)
            out[h, k : k + rows, :inner] = parted[:rows]
            out[h, k : k + rows, inner:] = parted[rows:]


def first_kernel(base, rows, held, gate_up, out, wbuf, spread, sem):
    per = held.shape[0]
    rest = wbuf.shape[0]
    _, most, width = rows.shape
    inner = out.shape[2] // 2
    copies = [pltpu.make_async_copy(gate_up.at[base + h], wbuf.at[h], sem.at[h]) for h in range(rest)]
    for copy in copies:
        copy.start()
    lane = 128
    src = lax.broadcasted_iota(jnp.int32, (lane, 4 * lane), 0)
    dst = lax.broadcasted_iota(jnp.int32, (lane, 4 * lane), 1)
    place = ((dst == 2 * src) | (dst == 2 * src + 1 + 2 * lane)).astype(F32).astype(BF16)
    for e in range(rest // 2):
        mine = rows[per // 2 + e]
        stacked = jnp.concatenate([mine[:, c : c + lane] for c in range(0, width, lane)], axis=0)
        both = jnp.dot(stacked, place, preferred_element_type=F32).astype(BF16)
        for c in range(width // lane):
            at = slice(2 * lane * c, 2 * lane * (c + 1))
            spread[e, :most, at] = both[most * c : most * (c + 1), : 2 * lane]
            spread[e, most:, at] = both[most * c : most * (c + 1), 2 * lane :]
    for h in range(per):
        out[h] = jnp.dot(rows[h // 2], held[h], preferred_element_type=F32).astype(BF16)
    for h in range(rest):
        copies[h].wait()
        acc = jnp.dot(spread[h // 2], wbuf[h].reshape(2 * width, inner), preferred_element_type=F32)
        out[per + h, :, :inner] = acc[:most].astype(BF16)
        out[per + h, :, inner:] = acc[most:].astype(BF16)


def gated_hidden(own, other):
    pre = own.astype(F32) + other.astype(F32)
    inner = pre.shape[1] // 2
    gate, up = pre[:, :inner], pre[:, inner:]
    return (gate / (1.0 + jnp.exp(-gate)) * up).astype(BF16)


def second_near_kernel(own, other, down, pairs, wbuf, sem):
    experts = pairs.shape[0]
    copies = [
        pltpu.make_async_copy(down.at[pl.ds(2 * e, 2)], wbuf.at[pl.ds(2 * e, 2)], sem.at[e]) for e in range(experts)
    ]
    for copy in copies:
        copy.start()
    for e in range(experts):
        hidden = [gated_hidden(own[h], other[h]) for h in (2 * e, 2 * e + 1)]
        copies[e].wait()
        acc = jnp.dot(hidden[0], wbuf[2 * e], preferred_element_type=F32)
        acc += jnp.dot(hidden[1], wbuf[2 * e + 1], preferred_element_type=F32)
        pairs[e] = acc.astype(BF16)


def second_far_kernel(base, chunk, width, *refs):
    if len(refs) == 5 + NR + 4:
        own, other, near_pairs, mix, down, hidden = refs[:6]
        outs = refs[6 : 6 + NR]
    else:
        hidden, near_pairs, mix, down = refs[:4]
        outs = refs[4 : 4 + NR]
        own = None
    pairs, wbuf, sem = refs[-3:]
    experts = pairs.shape[0]
    at = chunk * width
    copies = [
        pltpu.make_async_copy(
            down.at[pl.ds(base + 2 * e, 2), :, pl.ds(at, width)], wbuf.at[pl.ds(2 * e, 2)], sem.at[e]
        )
        for e in range(experts)
    ]
    for copy in copies:
        copy.start()
    if own is not None:
        for h in range(2 * experts):
            hidden[h] = gated_hidden(own[h], other[h])
    for e in range(experts):
        copies[e].wait()
        acc = jnp.dot(hidden[2 * e], wbuf[2 * e], preferred_element_type=F32)
        acc += jnp.dot(hidden[2 * e + 1], wbuf[2 * e + 1], preferred_element_type=F32)
        pairs[e] = acc.astype(BF16)
    dims = (((0,), (0,)), ((), ()))
    near = near_pairs.shape[0]
    for q in range(NR):
        span = slice(q * CAP, (q + 1) * CAP)
        rows = jnp.concatenate([near_pairs[:, span, at : at + width], pairs[:, span, :]], axis=0)
        rows = rows.reshape((near + experts) * CAP, width)
        total = lax.dot_general(mix[q, 0], rows, dims, preferred_element_type=F32)
        total += lax.dot_general(mix[q, 1], rows, dims, preferred_element_type=F32)
        outs[q][...] = total.astype(BF16)


def split3(values):
    high = values.astype(BF16)
    rest = values - high.astype(F32)
    middle = rest.astype(BF16)
    return high, middle, (rest - middle.astype(F32)).astype(BF16)


def on_device_ring(
    tile_hidden, cached_rows, tile_image, cache_ids, adapter_weight, routes, route_gates, gate_up, expert_down
):
    slots, tile_rows, adapt_width = tile_hidden.shape
    toks = slots * tile_rows
    half_width = cached_rows.shape[1]
    halves, _, _, inner = gate_up.shape
    experts = halves // 2
    shard = adapter_weight.shape[0]
    params = pltpu.CompilerParams(vmem_limit_bytes=VMEM_LIMIT)

    def message():
        cache_hit = jnp.any(tile_image[:, None] == cache_ids[None, :], axis=1)
        tokens_own = jnp.where(
            cache_hit[:, None, None], cached_rows.reshape(slots, tile_rows, half_width), activate(tile_hidden)
        ).reshape(toks, half_width)
        flags = jnp.broadcast_to(jnp.where(cache_hit, 0.0, 1.0).astype(BF16)[:, None], (slots, toks))
        info_own = jnp.concatenate([routes.T.astype(BF16), flags, jnp.zeros((16 - TOP - slots, toks), BF16)])
        gates = [jnp.pad(piece, ((0, 16 - TOP), (0, 0))) for piece in split3(route_gates.T)]
        info_own = jnp.concatenate([info_own] + gates, axis=1)
        info_own = jnp.pad(info_own, ((0, 0), (0, half_width - 4 * toks)))
        return jnp.concatenate([tokens_own, info_own])

    def fetch(base, count, limit):
        shape = (count, half_width, 2 * inner)
        return pl.pallas_call(
            functools.partial(fetch_kernel, base),
            in_specs=[ANY],
            out_specs=VM,
            out_shape=jax.ShapeDtypeStruct(shape, BF16),
            scratch_shapes=[
                pltpu.VMEM((count, half_width, 2, inner), BF16),
                pltpu.SemaphoreType.DMA((count,)),
            ],
            compiler_params=pltpu.CompilerParams(vmem_limit_bytes=limit << 20),
            cost_estimate=pl.CostEstimate(
                flops=512 * count * half_width * 2 * inner, bytes_accessed=8 * count * half_width * inner, transcendentals=0
            ),
        )(gate_up)

    near = experts // 2
    far = experts - near
    count = halves // 4
    fetches = [functools.partial(fetch, i * count, count, limit) for i, limit in enumerate(FETCH_LIMITS)]
    part = shard // 2
    weight_part = jnp.where(lax.axis_index("grp") == 0, adapter_weight[:part], adapter_weight[part:])
    weight_ring, sent, fetched, weight_across = ring_gather_two(weight_part, message, fetches)
    weight_in = [adapter_weight, *weight_ring[1:], *weight_across]
    *fetched_near, fetched_far = fetched
    most = NR * CAP
    pre_shape = jax.ShapeDtypeStruct((2 * near, most, 2 * inner), BF16)
    rows, mix, own_near = pl.pallas_call(
        functools.partial(prologue_kernel, experts, slots, tile_rows),
        in_specs=[VM] * (NR + len(weight_in)) + [VM] * len(fetched_near),
        out_specs=[VM, VM, VM],
        out_shape=[
            jax.ShapeDtypeStruct((far, most, half_width), BF16),
            jax.ShapeDtypeStruct((NR, 2, experts * CAP, toks), BF16),
            pre_shape,
        ],
        scratch_shapes=[
            pltpu.VMEM((NR, toks + 16, half_width), BF16),
            pltpu.VMEM((NR * shard, half_width), BF16),
            pltpu.VMEM((NR * slots // 2, tile_rows, half_width), BF16),
            pltpu.VMEM((near, most, half_width), BF16),
            pltpu.SMEM((NR * slots,), jnp.int32),
        ],
        compiler_params=pltpu.CompilerParams(vmem_limit_bytes=VMEM_SMALL),
    )(*sent, *weight_in, *fetched_near)
    other_near = swap(own_near, "narrow")

    own_far = pl.pallas_call(
        functools.partial(first_kernel, 3 * count),
        in_specs=[VM, VM, ANY],
        out_specs=VM,
        out_shape=jax.ShapeDtypeStruct((2 * far, most, 2 * inner), BF16),
        scratch_shapes=[
            pltpu.VMEM((count, half_width, 2, inner), BF16),
            pltpu.VMEM((count // 2, 2 * most, 2 * half_width), BF16),
            pltpu.SemaphoreType.DMA((count,)),
        ],
        compiler_params=pltpu.CompilerParams(vmem_limit_bytes=VMEM_FAR),
        cost_estimate=pl.CostEstimate(
            flops=16 * most * half_width * far * inner, bytes_accessed=8 * far * half_width * inner, transcendentals=0
        ),
    )(rows, fetched_far, gate_up)
    own_far, other_near = tie(own_far, other_near)
    other_far = swap(own_far, "narrow")

    near_pairs = pl.pallas_call(
        second_near_kernel,
        in_specs=[VM, VM, ANY],
        out_specs=VM,
        out_shape=jax.ShapeDtypeStruct((near, most, half_width), BF16),
        scratch_shapes=[pltpu.VMEM((2 * near, inner, half_width), BF16), pltpu.SemaphoreType.DMA((near,))],
        compiler_params=params,
        cost_estimate=pl.CostEstimate(
            flops=4 * near * most * inner * half_width,
            bytes_accessed=4 * near * inner * half_width,
            transcendentals=2 * near * most * inner,
        ),
    )(own_near, other_near, expert_down)
    near_pairs, other_far = tie(near_pairs, other_far)

    n_second = 2
    width = half_width // n_second
    mixed = []
    hidden = None
    for c in range(n_second):
        start = hidden is None
        out = pl.pallas_call(
            functools.partial(second_far_kernel, 2 * near, c, width),
            in_specs=[VM] * (4 if start else 3) + [ANY],
            out_specs=[VM] * (start + NR),
            out_shape=[jax.ShapeDtypeStruct((2 * far, most, inner), BF16)] * start
            + [jax.ShapeDtypeStruct((toks, width), BF16)] * NR,
            scratch_shapes=[
                pltpu.VMEM((far, most, width), BF16),
                pltpu.VMEM((2 * far, inner, width), BF16),
                pltpu.SemaphoreType.DMA((far,)),
            ],
            compiler_params=params,
            cost_estimate=pl.CostEstimate(
                flops=4 * far * most * inner * width, bytes_accessed=4 * far * inner * width, transcendentals=0
            ),
        )(*((own_far, other_far) if start else (hidden,)), near_pairs, mix, expert_down)
        if start:
            hidden, *out = out
        mixed.append(ring_scatter(out, c % 2 == 0))
    return jnp.concatenate(mixed, axis=1)


def solution(mesh):
    body = on_device_ring if mesh.shape["wide"] == NR else on_device_plain
    return jax.shard_map(
        body,
        mesh=mesh,
        in_specs=(
            P(("grp", "wide"), None, None),
            P(("grp", "wide"), "narrow"),
            P(("grp", "wide")),
            P("grp"),
            P("wide", "narrow"),
            P(("grp", "wide"), None),
            P(("grp", "wide"), None),
            P("wide", "narrow", None, None),
            P("wide", None, "narrow"),
        ),
        out_specs=P(("grp", "wide"), "narrow"),
        check_vma=False,
    )
```

```python
import functools
import math

import jax
import jax.numpy as jnp
from jax import lax
from jax.experimental import pallas as pl
from jax.experimental.pallas import tpu as pltpu
from jax.sharding import PartitionSpec as P

EXPERTS = 64
TOP = 6
CAP = 16
F32 = jnp.float32
BF16 = jnp.bfloat16
RING = (0, 2, 4, 6, 7, 5, 3, 1)
NR = 8
CROSSING = ((1, 7, 2, 6), (3, 5), (4,))
VMEM_LIMIT = 43 << 20
VMEM_SMALL = 10 << 20
VMEM_FAR = 25 << 20
FETCH_LIMITS = (34, 26, 18)
ANY = pl.BlockSpec(memory_space=pl.ANY)
VM = pl.BlockSpec(memory_space=pltpu.VMEM)


def activate(tiles):
    return jax.nn.gelu(tiles.astype(F32), approximate=False).astype(BF16)


def round_keep(values):
    return lax.optimization_barrier(values.astype(BF16)).astype(F32)


def on_device_plain(
    tile_hidden, cached_rows, tile_image, cache_ids, adapter_weight, routes, route_gates, gate_up, expert_down
):
    slot_count, tile_rows, adapt_width = tile_hidden.shape
    half_width = cached_rows.shape[1]
    cache_hit = jnp.any(tile_image[:, None] == cache_ids[None, :], axis=1)
    whole_weight = lax.all_gather(adapter_weight, "wide", axis=0, tiled=True)
    active = activate(tile_hidden).reshape(slot_count * tile_rows, adapt_width)
    encoded = jnp.dot(active, whole_weight, preferred_element_type=F32).astype(BF16)
    token_count = slot_count * tile_rows
    hit_rows = jnp.repeat(cache_hit, tile_rows)
    tokens_in = jnp.where(hit_rows[:, None], cached_rows, encoded)
    expert_flat = routes.reshape(-1)
    pair_count = expert_flat.shape[0]
    onehot = (expert_flat[:, None] == jnp.arange(EXPERTS, dtype=jnp.int32)[None, :]).astype(jnp.int32)
    earlier = jnp.cumsum(onehot, axis=0) - onehot
    slot_index = jnp.sum(earlier * onehot, axis=1)
    target = expert_flat * CAP + slot_index
    owner_table = (
        jnp.full((EXPERTS * CAP,), token_count, jnp.int32)
        .at[target]
        .set(jnp.arange(pair_count, dtype=jnp.int32) // TOP)
    )
    padded_tokens = jnp.concatenate([tokens_in, jnp.zeros((1, half_width), BF16)])
    expert_rows = padded_tokens[owner_table].reshape(EXPERTS, CAP, half_width)
    local_halves = gate_up.shape[0]
    outgoing = jnp.broadcast_to(expert_rows[:, None], (EXPERTS, 2, CAP, half_width)).reshape(
        2 * EXPERTS, CAP, half_width
    )
    arrived = lax.all_to_all(outgoing, "wide", split_axis=0, concat_axis=1, tiled=True)
    inner_width = gate_up.shape[3]
    preact_local = jnp.einsum(
        "lrd,ldf->lrf",
        arrived,
        gate_up.reshape(local_halves, half_width, 2 * inner_width),
        preferred_element_type=F32,
    )
    rounded = round_keep(preact_local)
    summed = lax.psum(rounded.astype(BF16), "narrow").astype(F32)
    hidden = (jax.nn.silu(summed[:, :, :inner_width]) * summed[:, :, inner_width:]).astype(BF16)
    partial_out = jnp.einsum("lrf,lfd->lrd", hidden, expert_down, preferred_element_type=F32).astype(BF16)
    returned = lax.all_to_all(partial_out, "wide", split_axis=1, concat_axis=0, tiled=True)
    both_halves = returned.reshape(EXPERTS, 2, CAP, half_width).astype(F32)
    summed_rows = round_keep(both_halves[:, 0] + both_halves[:, 1]).reshape(EXPERTS * CAP, half_width)
    picked = summed_rows[target].reshape(token_count, TOP, half_width)
    mixed = jnp.sum(picked * route_gates[:, :, None], axis=1)
    return mixed.astype(BF16)


def ring_pairs(shift):
    return [(RING[i], RING[(i + shift) % NR]) for i in range(NR)]


def from_prev(value):
    return lax.ppermute(value, "wide", ring_pairs(1))


def from_next(value):
    return lax.ppermute(value, "wide", ring_pairs(-1))


def swap(value, axis):
    return lax.ppermute(value, axis, [(0, 1), (1, 0)])


def tie(*values):
    return lax.optimization_barrier(values)


def ring_gather_two(first, make_second, fetches):
    one, two = [first] * NR, [None] * NR
    fetched, across = [], []
    far = NR // 2
    for q in range(1, far + 1):
        up, down = one[q - 1], one[(NR - q + 1) % NR]
        if q > 2:
            up, down, two[q - 2], two[NR - q + 2] = tie(up, down, two[q - 2], two[NR - q + 2])
        if q < far:
            one[q], one[NR - q] = from_prev(up), from_next(down)
        else:
            one[q] = from_next(down)
        if q == 1:
            two[0], one[1], one[NR - 1] = tie(make_second(), one[1], one[NR - 1])
        up, down = two[q - 1], two[(NR - q + 1) % NR]
        if 1 < q < far:
            up, down, one[q], one[NR - q], *fetched = tie(up, down, one[q], one[NR - q], *fetched)
        elif q == far:
            up, two[NR - q + 1], one[q], across[0], across[1], *fetched = tie(up, two[NR - q + 1], one[q], *across, *fetched)
        if q < far:
            two[q], two[NR - q] = from_prev(up), from_next(down)
            if fetches:
                fetched.append(fetches.pop(0)())
        else:
            two[q] = from_prev(up)
        if q == far // 2:
            across.append(swap(jnp.concatenate([one[p] for p in CROSSING[0]]), "grp"))
        elif q > far // 2:
            pieces = [one[p] for p in CROSSING[q - far // 2]]
            across.append(swap(jnp.concatenate(pieces) if len(pieces) > 1 else pieces[0], "grp"))
    return one, two, fetched, across


def add(left, right):
    return (left.astype(F32) + right.astype(F32)).astype(BF16)


def ring_scatter(parts, antipode_by_next):
    if antipode_by_next:
        low = add(from_next(parts[4]), parts[3])
        high = parts[5]
    else:
        low = parts[3]
        high = add(from_prev(parts[4]), parts[5])
    for q in (2, 1, 0):
        low = from_next(low)
        high = from_prev(high)
        if q:
            low = add(low, parts[q])
            high = add(high, parts[NR - q])
    return (parts[0].astype(F32) + low.astype(F32) + high.astype(F32)).astype(BF16)


def ring_source(q):
    wide_id = lax.axis_index("wide")
    level = wide_id // 2
    pos = jnp.where(wide_id % 2 == 1, NR - 1 - level, level)
    pos = (pos + NR - q) % NR
    return jnp.where(pos < NR // 2, 2 * pos, 2 * (NR - 1 - pos) + 1)


def prologue_kernel(experts, slots, tile_rows, *refs):
    toks = slots * tile_rows
    sent_in = refs[:NR]
    weight_own, weight_ring = refs[NR], refs[NR + 1 : 2 * NR]
    weight_across = refs[2 * NR : 2 * NR + len(CROSSING)]
    gate_up = refs[2 * NR + len(CROSSING) : -8]
    rows_out, mix_out, pre_out, sent, weight, packed, rows_here, missed_at = refs[-8:]
    near = rows_here.shape[0]
    shard = weight_own.shape[0]
    part = shard // 2
    width = packed.shape[2]
    grp_id = lax.axis_index("grp")
    pieces = [(weight_own, 0, 0, shard)]
    for q in range(1, NR):
        pieces.append((weight_ring[q - 1], q, grp_id * part, part))
    for batch, group in zip(weight_across, CROSSING):
        for i, q in enumerate(group):
            pieces.append((batch.at[pl.ds(i * part, part)], q, (1 - grp_id) * part, part))
    for q, ref in enumerate(sent_in):
        sent[q] = ref[...]
    for ref, q, begin, count in pieces:
        at = pl.multiple_of(ring_source(q) * shard + begin, part)
        weight[pl.ds(at, count)] = ref[...]

    first = (lax.axis_index("wide") * experts).astype(F32)
    before = lax.broadcasted_iota(jnp.int32, (toks, toks), 0) < lax.broadcasted_iota(jnp.int32, (toks, toks), 1)
    before = before.astype(F32).astype(BF16)
    ids = lax.broadcasted_iota(jnp.int32, (experts, toks), 0).astype(F32) + first
    place = lax.broadcasted_iota(jnp.int32, (experts, CAP, toks), 1).astype(F32)
    picks = []
    missed = jnp.int32(0)
    for q in range(NR):
        info = sent[q, toks:].astype(F32)
        for s in range(slots):
            flag = info[TOP + s, 0] > 0.5
            missed_at[missed] = q * slots + s
            missed = missed + flag.astype(jnp.int32)
        named = jnp.zeros((experts, toks), F32)
        gate = jnp.zeros((experts, toks), F32)
        for k in range(TOP):
            same = jnp.broadcast_to(info[k : k + 1, :toks], (experts, toks)) == ids
            named = jnp.where(same, 1.0, named)
            value = info[k : k + 1, toks : 2 * toks] + info[k : k + 1, 2 * toks : 3 * toks]
            value = value + info[k : k + 1, 3 * toks : 4 * toks]
            gate = jnp.where(same, jnp.broadcast_to(value, (experts, toks)), gate)
        rank = jnp.dot(named.astype(BF16), before, preferred_element_type=F32)
        rank = jnp.where(named > 0.0, rank, -1.0)
        chosen = jnp.broadcast_to(rank[:, None, :], (experts, CAP, toks)) == place
        pick = jnp.where(chosen, 1.0, 0.0).reshape(experts * CAP, toks)
        picks.append(pick.astype(BF16))
        gated = jnp.where(chosen, jnp.broadcast_to(gate[:, None, :], (experts, CAP, toks)), 0.0)
        gated = gated.reshape(experts * CAP, toks)
        coarse = gated.astype(BF16)
        mix_out[q, 0] = coarse
        mix_out[q, 1] = (gated - coarse.astype(F32)).astype(BF16)

    most = packed.shape[0]

    def tile_of(i):
        n = missed_at[i]
        return sent.at[n // slots, pl.ds(pl.multiple_of((n % slots) * tile_rows, tile_rows), tile_rows)]

    for i in range(most):

        @pl.when(i < missed)
        def _(i=i):
            packed[i] = tile_of(i)[...]

    group = 4
    for i in range(0, most, group):

        @pl.when(i < missed)
        def _(i=i):
            rows = packed[i : i + group].reshape(group * tile_rows, width)
            coded = jnp.dot(rows, weight[...], preferred_element_type=F32).astype(BF16)
            for j in range(group):

                @pl.when(i + j < missed)
                def _(j=j):
                    tile_of(i + j)[...] = coded[j * tile_rows : (j + 1) * tile_rows]

    for q in range(NR):
        rows = jnp.dot(picks[q], sent[q, :toks], preferred_element_type=F32).astype(BF16)
        rows = rows.reshape(experts, CAP, width)
        rows_here[:, q * CAP : (q + 1) * CAP, :] = rows[:near]
        rows_out[:, q * CAP : (q + 1) * CAP, :] = rows[near:]
    first_matmuls(rows_here, gate_up, pre_out)


def first_matmuls(rows, weights, out):
    per = weights[0].shape[0]
    for h in range(out.shape[0]):
        out[h] = jnp.dot(rows[h // 2], weights[h // per][h % per], preferred_element_type=F32).astype(BF16)


def fetch_kernel(base, gate_up, out, buf, sem):
    halves, width, _ = out.shape
    inner = gate_up.shape[3]
    copies = [pltpu.make_async_copy(gate_up.at[base + h], buf.at[h], sem.at[h]) for h in range(halves)]
    for copy in copies:
        copy.start()
    rows = 128
    dst = lax.broadcasted_iota(jnp.int32, (2 * rows, 2 * rows), 0)
    src = lax.broadcasted_iota(jnp.int32, (2 * rows, 2 * rows), 1)
    parting = (src == jnp.where(dst < rows, 2 * dst, 2 * (dst - rows) + 1)).astype(F32).astype(BF16)
    for h in range(halves):
        copies[h].wait()
        for k in range(0, width, rows):
            mixed = buf[h, k : k + rows].reshape(2 * rows, inner)
            parted = jnp.dot(parting, mixed, preferred_element_type=F32).astype(BF16)
            out[h, k : k + rows, :inner] = parted[:rows]
            out[h, k : k + rows, inner:] = parted[rows:]


def first_kernel(base, rows, held, gate_up, out, wbuf, spread, sem):
    per = held.shape[0]
    rest = wbuf.shape[0]
    _, most, width = rows.shape
    inner = out.shape[2] // 2
    copies = [pltpu.make_async_copy(gate_up.at[base + h], wbuf.at[h], sem.at[h]) for h in range(rest)]
    for copy in copies:
        copy.start()
    lane = 128
    src = lax.broadcasted_iota(jnp.int32, (lane, 4 * lane), 0)
    dst = lax.broadcasted_iota(jnp.int32, (lane, 4 * lane), 1)
    place = ((dst == 2 * src) | (dst == 2 * src + 1 + 2 * lane)).astype(F32).astype(BF16)
    for e in range(rest // 2):
        mine = rows[per // 2 + e]
        stacked = jnp.concatenate([mine[:, c : c + lane] for c in range(0, width, lane)], axis=0)
        both = jnp.dot(stacked, place, preferred_element_type=F32).astype(BF16)
        for c in range(width // lane):
            at = slice(2 * lane * c, 2 * lane * (c + 1))
            spread[e, :most, at] = both[most * c : most * (c + 1), : 2 * lane]
            spread[e, most:, at] = both[most * c : most * (c + 1), 2 * lane :]
    for h in range(per):
        out[h] = jnp.dot(rows[h // 2], held[h], preferred_element_type=F32).astype(BF16)
    for h in range(rest):
        copies[h].wait()
        acc = jnp.dot(spread[h // 2], wbuf[h].reshape(2 * width, inner), preferred_element_type=F32)
        out[per + h, :, :inner] = acc[:most].astype(BF16)
        out[per + h, :, inner:] = acc[most:].astype(BF16)


def gated_hidden(own, other):
    pre = own.astype(F32) + other.astype(F32)
    inner = pre.shape[1] // 2
    gate, up = pre[:, :inner], pre[:, inner:]
    return (gate / (1.0 + jnp.exp(-gate)) * up).astype(BF16)


def second_near_kernel(own, other, down, pairs, wbuf, sem):
    experts = pairs.shape[0]
    copies = [
        pltpu.make_async_copy(down.at[pl.ds(2 * e, 2)], wbuf.at[pl.ds(2 * e, 2)], sem.at[e]) for e in range(experts)
    ]
    for copy in copies:
        copy.start()
    for e in range(experts):
        hidden = [gated_hidden(own[h], other[h]) for h in (2 * e, 2 * e + 1)]
        copies[e].wait()
        acc = jnp.dot(hidden[0], wbuf[2 * e], preferred_element_type=F32)
        acc += jnp.dot(hidden[1], wbuf[2 * e + 1], preferred_element_type=F32)
        pairs[e] = acc.astype(BF16)


def second_far_kernel(base, chunk, width, *refs):
    if len(refs) == 5 + NR + 4:
        own, other, near_pairs, mix, down, hidden = refs[:6]
        outs = refs[6 : 6 + NR]
    else:
        hidden, near_pairs, mix, down = refs[:4]
        outs = refs[4 : 4 + NR]
        own = None
    pairs, wbuf, sem = refs[-3:]
    experts = pairs.shape[0]
    at = chunk * width
    copies = [
        pltpu.make_async_copy(
            down.at[pl.ds(base + 2 * e, 2), :, pl.ds(at, width)], wbuf.at[pl.ds(2 * e, 2)], sem.at[e]
        )
        for e in range(experts)
    ]
    for copy in copies:
        copy.start()
    if own is not None:
        for h in range(2 * experts):
            hidden[h] = gated_hidden(own[h], other[h])
    for e in range(experts):
        copies[e].wait()
        acc = jnp.dot(hidden[2 * e], wbuf[2 * e], preferred_element_type=F32)
        acc += jnp.dot(hidden[2 * e + 1], wbuf[2 * e + 1], preferred_element_type=F32)
        pairs[e] = acc.astype(BF16)
    dims = (((0,), (0,)), ((), ()))
    near = near_pairs.shape[0]
    for q in range(NR):
        span = slice(q * CAP, (q + 1) * CAP)
        rows = jnp.concatenate([near_pairs[:, span, at : at + width], pairs[:, span, :]], axis=0)
        rows = rows.reshape((near + experts) * CAP, width)
        total = lax.dot_general(mix[q, 0], rows, dims, preferred_element_type=F32)
        total += lax.dot_general(mix[q, 1], rows, dims, preferred_element_type=F32)
        outs[q][...] = total.astype(BF16)


def split3(values):
    high = values.astype(BF16)
    rest = values - high.astype(F32)
    middle = rest.astype(BF16)
    return high, middle, (rest - middle.astype(F32)).astype(BF16)


def on_device_ring(
    tile_hidden, cached_rows, tile_image, cache_ids, adapter_weight, routes, route_gates, gate_up, expert_down
):
    slots, tile_rows, adapt_width = tile_hidden.shape
    toks = slots * tile_rows
    half_width = cached_rows.shape[1]
    halves, _, _, inner = gate_up.shape
    experts = halves // 2
    shard = adapter_weight.shape[0]
    params = pltpu.CompilerParams(vmem_limit_bytes=VMEM_LIMIT)

    def message():
        cache_hit = jnp.any(tile_image[:, None] == cache_ids[None, :], axis=1)
        tokens_own = jnp.where(
            cache_hit[:, None, None], cached_rows.reshape(slots, tile_rows, half_width), activate(tile_hidden)
        ).reshape(toks, half_width)
        flags = jnp.broadcast_to(jnp.where(cache_hit, 0.0, 1.0).astype(BF16)[:, None], (slots, toks))
        info_own = jnp.concatenate([routes.T.astype(BF16), flags, jnp.zeros((16 - TOP - slots, toks), BF16)])
        gates = [jnp.pad(piece, ((0, 16 - TOP), (0, 0))) for piece in split3(route_gates.T)]
        info_own = jnp.concatenate([info_own] + gates, axis=1)
        info_own = jnp.pad(info_own, ((0, 0), (0, half_width - 4 * toks)))
        return jnp.concatenate([tokens_own, info_own])

    def fetch(base, count, limit):
        shape = (count, half_width, 2 * inner)
        return pl.pallas_call(
            functools.partial(fetch_kernel, base),
            in_specs=[ANY],
            out_specs=VM,
            out_shape=jax.ShapeDtypeStruct(shape, BF16),
            scratch_shapes=[
                pltpu.VMEM((count, half_width, 2, inner), BF16),
                pltpu.SemaphoreType.DMA((count,)),
            ],
            compiler_params=pltpu.CompilerParams(vmem_limit_bytes=limit << 20),
            cost_estimate=pl.CostEstimate(
                flops=512 * count * half_width * 2 * inner, bytes_accessed=8 * count * half_width * inner, transcendentals=0
            ),
        )(gate_up)

    near = experts // 2
    far = experts - near
    count = halves // 4
    fetches = [functools.partial(fetch, i * count, count, limit) for i, limit in enumerate(FETCH_LIMITS)]
    part = shard // 2
    weight_part = jnp.where(lax.axis_index("grp") == 0, adapter_weight[:part], adapter_weight[part:])
    weight_ring, sent, fetched, weight_across = ring_gather_two(weight_part, message, fetches)
    weight_in = [adapter_weight, *weight_ring[1:], *weight_across]
    *fetched_near, fetched_far = fetched
    most = NR * CAP
    pre_shape = jax.ShapeDtypeStruct((2 * near, most, 2 * inner), BF16)
    rows, mix, own_near = pl.pallas_call(
        functools.partial(prologue_kernel, experts, slots, tile_rows),
        in_specs=[VM] * (NR + len(weight_in)) + [VM] * len(fetched_near),
        out_specs=[VM, VM, VM],
        out_shape=[
            jax.ShapeDtypeStruct((far, most, half_width), BF16),
            jax.ShapeDtypeStruct((NR, 2, experts * CAP, toks), BF16),
            pre_shape,
        ],
        scratch_shapes=[
            pltpu.VMEM((NR, toks + 16, half_width), BF16),
            pltpu.VMEM((NR * shard, half_width), BF16),
            pltpu.VMEM((NR * slots // 2, tile_rows, half_width), BF16),
            pltpu.VMEM((near, most, half_width), BF16),
            pltpu.SMEM((NR * slots,), jnp.int32),
        ],
        compiler_params=pltpu.CompilerParams(vmem_limit_bytes=VMEM_SMALL),
    )(*sent, *weight_in, *fetched_near)
    other_near = swap(own_near, "narrow")

    own_far = pl.pallas_call(
        functools.partial(first_kernel, 3 * count),
        in_specs=[VM, VM, ANY],
        out_specs=VM,
        out_shape=jax.ShapeDtypeStruct((2 * far, most, 2 * inner), BF16),
        scratch_shapes=[
            pltpu.VMEM((count, half_width, 2, inner), BF16),
            pltpu.VMEM((count // 2, 2 * most, 2 * half_width), BF16),
            pltpu.SemaphoreType.DMA((count,)),
        ],
        compiler_params=pltpu.CompilerParams(vmem_limit_bytes=VMEM_FAR),
        cost_estimate=pl.CostEstimate(
            flops=16 * most * half_width * far * inner, bytes_accessed=8 * far * half_width * inner, transcendentals=0
        ),
    )(rows, fetched_far, gate_up)
    own_far, other_near = tie(own_far, other_near)
    other_far = swap(own_far, "narrow")

    near_pairs = pl.pallas_call(
        second_near_kernel,
        in_specs=[VM, VM, ANY],
        out_specs=VM,
        out_shape=jax.ShapeDtypeStruct((near, most, half_width), BF16),
        scratch_shapes=[pltpu.VMEM((2 * near, inner, half_width), BF16), pltpu.SemaphoreType.DMA((near,))],
        compiler_params=params,
        cost_estimate=pl.CostEstimate(
            flops=4 * near * most * inner * half_width,
            bytes_accessed=4 * near * inner * half_width,
            transcendentals=2 * near * most * inner,
        ),
    )(own_near, other_near, expert_down)
    near_pairs, other_far = tie(near_pairs, other_far)

    n_second = 2
    width = half_width // n_second
    mixed = []
    hidden = None
    for c in range(n_second):
        start = hidden is None
        out = pl.pallas_call(
            functools.partial(second_far_kernel, 2 * near, c, width),
            in_specs=[VM] * (4 if start else 3) + [ANY],
            out_specs=[VM] * (start + NR),
            out_shape=[jax.ShapeDtypeStruct((2 * far, most, inner), BF16)] * start
            + [jax.ShapeDtypeStruct((toks, width), BF16)] * NR,
            scratch_shapes=[
                pltpu.VMEM((far, most, width), BF16),
                pltpu.VMEM((2 * far, inner, width), BF16),
                pltpu.SemaphoreType.DMA((far,)),
            ],
            compiler_params=params,
            cost_estimate=pl.CostEstimate(
                flops=4 * far * most * inner * width, bytes_accessed=4 * far * inner * width, transcendentals=0
            ),
        )(*((own_far, other_far) if start else (hidden,)), near_pairs, mix, expert_down)
        if start:
            hidden, *out = out
        mixed.append(ring_scatter(out, c % 2 == 0))
    return jnp.concatenate(mixed, axis=1)


def solution(mesh):
    body = on_device_ring if mesh.shape["wide"] == NR else on_device_plain
    return jax.shard_map(
        body,
        mesh=mesh,
        in_specs=(
            P(("grp", "wide"), None, None),
            P(("grp", "wide"), "narrow"),
            P(("grp", "wide")),
            P("grp"),
            P("wide", "narrow"),
            P(("grp", "wide"), None),
            P(("grp", "wide"), None),
            P("wide", "narrow", None, None),
            P("wide", None, "narrow"),
        ),
        out_specs=P(("grp", "wide"), "narrow"),
        check_vma=False,
    )
```

```python
import functools
import math

import jax
import jax.numpy as jnp
from jax import lax
from jax.experimental import pallas as pl
from jax.experimental.pallas import tpu as pltpu
from jax.sharding import PartitionSpec as P

EXPERTS = 64
TOP = 6
CAP = 16
F32 = jnp.float32
BF16 = jnp.bfloat16
RING = (0, 2, 4, 6, 7, 5, 3, 1)
NR = 8
CROSSING = ((1, 7, 2, 6), (3, 5), (4,))
VMEM_LIMIT = 43 << 20
VMEM_SMALL = 10 << 20
VMEM_FAR = 25 << 20
FETCH_LIMITS = (34, 26, 18)
ANY = pl.BlockSpec(memory_space=pl.ANY)
VM = pl.BlockSpec(memory_space=pltpu.VMEM)


def activate(tiles):
    return jax.nn.gelu(tiles.astype(F32), approximate=False).astype(BF16)


def round_keep(values):
    return lax.optimization_barrier(values.astype(BF16)).astype(F32)


def on_device_plain(
    tile_hidden, cached_rows, tile_image, cache_ids, adapter_weight, routes, route_gates, gate_up, expert_down
):
    slot_count, tile_rows, adapt_width = tile_hidden.shape
    half_width = cached_rows.shape[1]
    cache_hit = jnp.any(tile_image[:, None] == cache_ids[None, :], axis=1)
    whole_weight = lax.all_gather(adapter_weight, "wide", axis=0, tiled=True)
    active = activate(tile_hidden).reshape(slot_count * tile_rows, adapt_width)
    encoded = jnp.dot(active, whole_weight, preferred_element_type=F32).astype(BF16)
    token_count = slot_count * tile_rows
    hit_rows = jnp.repeat(cache_hit, tile_rows)
    tokens_in = jnp.where(hit_rows[:, None], cached_rows, encoded)
    expert_flat = routes.reshape(-1)
    pair_count = expert_flat.shape[0]
    onehot = (expert_flat[:, None] == jnp.arange(EXPERTS, dtype=jnp.int32)[None, :]).astype(jnp.int32)
    earlier = jnp.cumsum(onehot, axis=0) - onehot
    slot_index = jnp.sum(earlier * onehot, axis=1)
    target = expert_flat * CAP + slot_index
    owner_table = (
        jnp.full((EXPERTS * CAP,), token_count, jnp.int32)
        .at[target]
        .set(jnp.arange(pair_count, dtype=jnp.int32) // TOP)
    )
    padded_tokens = jnp.concatenate([tokens_in, jnp.zeros((1, half_width), BF16)])
    expert_rows = padded_tokens[owner_table].reshape(EXPERTS, CAP, half_width)
    local_halves = gate_up.shape[0]
    outgoing = jnp.broadcast_to(expert_rows[:, None], (EXPERTS, 2, CAP, half_width)).reshape(
        2 * EXPERTS, CAP, half_width
    )
    arrived = lax.all_to_all(outgoing, "wide", split_axis=0, concat_axis=1, tiled=True)
    inner_width = gate_up.shape[3]
    preact_local = jnp.einsum(
        "lrd,ldf->lrf",
        arrived,
        gate_up.reshape(local_halves, half_width, 2 * inner_width),
        preferred_element_type=F32,
    )
    rounded = round_keep(preact_local)
    summed = lax.psum(rounded.astype(BF16), "narrow").astype(F32)
    hidden = (jax.nn.silu(summed[:, :, :inner_width]) * summed[:, :, inner_width:]).astype(BF16)
    partial_out = jnp.einsum("lrf,lfd->lrd", hidden, expert_down, preferred_element_type=F32).astype(BF16)
    returned = lax.all_to_all(partial_out, "wide", split_axis=1, concat_axis=0, tiled=True)
    both_halves = returned.reshape(EXPERTS, 2, CAP, half_width).astype(F32)
    summed_rows = round_keep(both_halves[:, 0] + both_halves[:, 1]).reshape(EXPERTS * CAP, half_width)
    picked = summed_rows[target].reshape(token_count, TOP, half_width)
    mixed = jnp.sum(picked * route_gates[:, :, None], axis=1)
    return mixed.astype(BF16)


def ring_pairs(shift):
    return [(RING[i], RING[(i + shift) % NR]) for i in range(NR)]


def from_prev(value):
    return lax.ppermute(value, "wide", ring_pairs(1))


def from_next(value):
    return lax.ppermute(value, "wide", ring_pairs(-1))


def swap(value, axis):
    return lax.ppermute(value, axis, [(0, 1), (1, 0)])


def tie(*values):
    return lax.optimization_barrier(values)


def ring_gather_two(first, make_second, fetches):
    one, two = [first] * NR, [None] * NR
    fetched, across = [], []
    far = NR // 2
    for q in range(1, far + 1):
        up, down = one[q - 1], one[(NR - q + 1) % NR]
        if q > 2:
            up, down, two[q - 2], two[NR - q + 2] = tie(up, down, two[q - 2], two[NR - q + 2])
        if q < far:
            one[q], one[NR - q] = from_prev(up), from_next(down)
        else:
            one[q] = from_next(down)
        if q == 1:
            two[0] = make_second()
        up, down = two[q - 1], two[(NR - q + 1) % NR]
        if 1 < q < far:
            up, down, one[q], one[NR - q], *fetched = tie(up, down, one[q], one[NR - q], *fetched)
        elif q == far:
            up, two[NR - q + 1], one[q], across[0], across[1], *fetched = tie(up, two[NR - q + 1], one[q], *across, *fetched)
        if q < far:
            two[q], two[NR - q] = from_prev(up), from_next(down)
            if fetches:
                fetched.append(fetches.pop(0)())
        else:
            two[q] = from_prev(up)
        if q == far // 2:
            across.append(swap(jnp.concatenate([one[p] for p in CROSSING[0]]), "grp"))
        elif q > far // 2:
            pieces = [one[p] for p in CROSSING[q - far // 2]]
            across.append(swap(jnp.concatenate(pieces) if len(pieces) > 1 else pieces[0], "grp"))
    return one, two, fetched, across


def add(left, right):
    return (left.astype(F32) + right.astype(F32)).astype(BF16)


def ring_scatter(parts, antipode_by_next):
    if antipode_by_next:
        low = add(from_next(parts[4]), parts[3])
        high = parts[5]
    else:
        low = parts[3]
        high = add(from_prev(parts[4]), parts[5])
    for q in (2, 1, 0):
        low = from_next(low)
        high = from_prev(high)
        if q:
            low = add(low, parts[q])
            high = add(high, parts[NR - q])
    return (parts[0].astype(F32) + low.astype(F32) + high.astype(F32)).astype(BF16)


def ring_source(q):
    wide_id = lax.axis_index("wide")
    level = wide_id // 2
    pos = jnp.where(wide_id % 2 == 1, NR - 1 - level, level)
    pos = (pos + NR - q) % NR
    return jnp.where(pos < NR // 2, 2 * pos, 2 * (NR - 1 - pos) + 1)


def prologue_kernel(experts, slots, tile_rows, *refs):
    toks = slots * tile_rows
    sent_in = refs[:NR]
    weight_own, weight_ring = refs[NR], refs[NR + 1 : 2 * NR]
    weight_across = refs[2 * NR : 2 * NR + len(CROSSING)]
    gate_up = refs[2 * NR + len(CROSSING) : -8]
    rows_out, mix_out, pre_out, sent, weight, packed, rows_here, missed_at = refs[-8:]
    near = rows_here.shape[0]
    shard = weight_own.shape[0]
    part = shard // 2
    width = packed.shape[2]
    grp_id = lax.axis_index("grp")
    pieces = [(weight_own, 0, 0, shard)]
    for q in range(1, NR):
        pieces.append((weight_ring[q - 1], q, grp_id * part, part))
    for batch, group in zip(weight_across, CROSSING):
        for i, q in enumerate(group):
            pieces.append((batch.at[pl.ds(i * part, part)], q, (1 - grp_id) * part, part))
    for q, ref in enumerate(sent_in):
        sent[q] = ref[...]
    for ref, q, begin, count in pieces:
        at = pl.multiple_of(ring_source(q) * shard + begin, part)
        weight[pl.ds(at, count)] = ref[...]

    first = (lax.axis_index("wide") * experts).astype(F32)
    before = lax.broadcasted_iota(jnp.int32, (toks, toks), 0) < lax.broadcasted_iota(jnp.int32, (toks, toks), 1)
    before = before.astype(F32).astype(BF16)
    ids = lax.broadcasted_iota(jnp.int32, (experts, toks), 0).astype(F32) + first
    place = lax.broadcasted_iota(jnp.int32, (experts, CAP, toks), 1).astype(F32)
    picks = []
    missed = jnp.int32(0)
    for q in range(NR):
        info = sent[q, toks:].astype(F32)
        for s in range(slots):
            flag = info[TOP + s, 0] > 0.5
            missed_at[missed] = q * slots + s
            missed = missed + flag.astype(jnp.int32)
        named = jnp.zeros((experts, toks), F32)
        gate = jnp.zeros((experts, toks), F32)
        for k in range(TOP):
            same = jnp.broadcast_to(info[k : k + 1, :toks], (experts, toks)) == ids
            named = jnp.where(same, 1.0, named)
            value = info[k : k + 1, toks : 2 * toks] + info[k : k + 1, 2 * toks : 3 * toks]
            value = value + info[k : k + 1, 3 * toks : 4 * toks]
            gate = jnp.where(same, jnp.broadcast_to(value, (experts, toks)), gate)
        rank = jnp.dot(named.astype(BF16), before, preferred_element_type=F32)
        rank = jnp.where(named > 0.0, rank, -1.0)
        chosen = jnp.broadcast_to(rank[:, None, :], (experts, CAP, toks)) == place
        pick = jnp.where(chosen, 1.0, 0.0).reshape(experts * CAP, toks)
        picks.append(pick.astype(BF16))
        gated = jnp.where(chosen, jnp.broadcast_to(gate[:, None, :], (experts, CAP, toks)), 0.0)
        gated = gated.reshape(experts * CAP, toks)
        coarse = gated.astype(BF16)
        mix_out[q, 0] = coarse
        mix_out[q, 1] = (gated - coarse.astype(F32)).astype(BF16)

    most = packed.shape[0]

    def tile_of(i):
        n = missed_at[i]
        return sent.at[n // slots, pl.ds(pl.multiple_of((n % slots) * tile_rows, tile_rows), tile_rows)]

    for i in range(most):

        @pl.when(i < missed)
        def _(i=i):
            packed[i] = tile_of(i)[...]

    group = 4
    for i in range(0, most, group):

        @pl.when(i < missed)
        def _(i=i):
            rows = packed[i : i + group].reshape(group * tile_rows, width)
            coded = jnp.dot(rows, weight[...], preferred_element_type=F32).astype(BF16)
            for j in range(group):

                @pl.when(i + j < missed)
                def _(j=j):
                    tile_of(i + j)[...] = coded[j * tile_rows : (j + 1) * tile_rows]

    for q in range(NR):
        rows = jnp.dot(picks[q], sent[q, :toks], preferred_element_type=F32).astype(BF16)
        rows = rows.reshape(experts, CAP, width)
        rows_here[:, q * CAP : (q + 1) * CAP, :] = rows[:near]
        rows_out[:, q * CAP : (q + 1) * CAP, :] = rows[near:]
    first_matmuls(rows_here, gate_up, pre_out)


def first_matmuls(rows, weights, out):
    per = weights[0].shape[0]
    for h in range(out.shape[0]):
        out[h] = jnp.dot(rows[h // 2], weights[h // per][h % per], preferred_element_type=F32).astype(BF16)


def fetch_kernel(base, gate_up, out, buf, sem):
    halves, width, _ = out.shape
    inner = gate_up.shape[3]
    copies = [pltpu.make_async_copy(gate_up.at[base + h], buf.at[h], sem.at[h]) for h in range(halves)]
    for copy in copies:
        copy.start()
    rows = 128
    dst = lax.broadcasted_iota(jnp.int32, (2 * rows, 2 * rows), 0)
    src = lax.broadcasted_iota(jnp.int32, (2 * rows, 2 * rows), 1)
    parting = (src == jnp.where(dst < rows, 2 * dst, 2 * (dst - rows) + 1)).astype(F32).astype(BF16)
    for h in range(halves):
        copies[h].wait()
        for k in range(0, width, rows):
            mixed = buf[h, k : k + rows].reshape(2 * rows, inner)
            parted = jnp.dot(parting, mixed, preferred_element_type=F32).astype(BF16)
            out[h, k : k + rows, :inner] = parted[:rows]
            out[h, k : k + rows, inner:] = parted[rows:]


def first_kernel(base, rows, held, gate_up, out, wbuf, spread, sem):
    per = held.shape[0]
    rest = wbuf.shape[0]
    _, most, width = rows.shape
    inner = out.shape[2] // 2
    copies = [pltpu.make_async_copy(gate_up.at[base + h], wbuf.at[h], sem.at[h]) for h in range(rest)]
    for copy in copies:
        copy.start()
    lane = 128
    src = lax.broadcasted_iota(jnp.int32, (lane, 4 * lane), 0)
    dst = lax.broadcasted_iota(jnp.int32, (lane, 4 * lane), 1)
    place = ((dst == 2 * src) | (dst == 2 * src + 1 + 2 * lane)).astype(F32).astype(BF16)
    for e in range(rest // 2):
        mine = rows[per // 2 + e]
        stacked = jnp.concatenate([mine[:, c : c + lane] for c in range(0, width, lane)], axis=0)
        both = jnp.dot(stacked, place, preferred_element_type=F32).astype(BF16)
        for c in range(width // lane):
            at = slice(2 * lane * c, 2 * lane * (c + 1))
            spread[e, :most, at] = both[most * c : most * (c + 1), : 2 * lane]
            spread[e, most:, at] = both[most * c : most * (c + 1), 2 * lane :]
    for h in range(per):
        out[h] = jnp.dot(rows[h // 2], held[h], preferred_element_type=F32).astype(BF16)
    for h in range(rest):
        copies[h].wait()
        acc = jnp.dot(spread[h // 2], wbuf[h].reshape(2 * width, inner), preferred_element_type=F32)
        out[per + h, :, :inner] = acc[:most].astype(BF16)
        out[per + h, :, inner:] = acc[most:].astype(BF16)


def gated_hidden(own, other):
    pre = own.astype(F32) + other.astype(F32)
    inner = pre.shape[1] // 2
    gate, up = pre[:, :inner], pre[:, inner:]
    return (gate / (1.0 + jnp.exp(-gate)) * up).astype(BF16)


def second_near_kernel(own, other, down, pairs, wbuf, sem):
    experts = pairs.shape[0]
    copies = [
        pltpu.make_async_copy(down.at[pl.ds(2 * e, 2)], wbuf.at[pl.ds(2 * e, 2)], sem.at[e]) for e in range(experts)
    ]
    for copy in copies:
        copy.start()
    for e in range(experts):
        hidden = [gated_hidden(own[h], other[h]) for h in (2 * e, 2 * e + 1)]
        copies[e].wait()
        acc = jnp.dot(hidden[0], wbuf[2 * e], preferred_element_type=F32)
        acc += jnp.dot(hidden[1], wbuf[2 * e + 1], preferred_element_type=F32)
        pairs[e] = acc.astype(BF16)


def second_far_kernel(base, chunk, width, *refs):
    if len(refs) == 5 + NR + 4:
        own, other, near_pairs, mix, down, hidden = refs[:6]
        outs = refs[6 : 6 + NR]
    else:
        hidden, near_pairs, mix, down = refs[:4]
        outs = refs[4 : 4 + NR]
        own = None
    pairs, wbuf, sem = refs[-3:]
    experts = pairs.shape[0]
    at = chunk * width
    copies = [
        pltpu.make_async_copy(
            down.at[pl.ds(base + 2 * e, 2), :, pl.ds(at, width)], wbuf.at[pl.ds(2 * e, 2)], sem.at[e]
        )
        for e in range(experts)
    ]
    for copy in copies:
        copy.start()
    if own is not None:
        for h in range(2 * experts):
            hidden[h] = gated_hidden(own[h], other[h])
    for e in range(experts):
        copies[e].wait()
        acc = jnp.dot(hidden[2 * e], wbuf[2 * e], preferred_element_type=F32)
        acc += jnp.dot(hidden[2 * e + 1], wbuf[2 * e + 1], preferred_element_type=F32)
        pairs[e] = acc.astype(BF16)
    dims = (((0,), (0,)), ((), ()))
    near = near_pairs.shape[0]
    for q in range(NR):
        span = slice(q * CAP, (q + 1) * CAP)
        rows = jnp.concatenate([near_pairs[:, span, at : at + width], pairs[:, span, :]], axis=0)
        rows = rows.reshape((near + experts) * CAP, width)
        total = lax.dot_general(mix[q, 0], rows, dims, preferred_element_type=F32)
        total += lax.dot_general(mix[q, 1], rows, dims, preferred_element_type=F32)
        outs[q][...] = total.astype(BF16)


def split3(values):
    high = values.astype(BF16)
    rest = values - high.astype(F32)
    middle = rest.astype(BF16)
    return high, middle, (rest - middle.astype(F32)).astype(BF16)


def on_device_ring(
    tile_hidden, cached_rows, tile_image, cache_ids, adapter_weight, routes, route_gates, gate_up, expert_down
):
    slots, tile_rows, adapt_width = tile_hidden.shape
    toks = slots * tile_rows
    half_width = cached_rows.shape[1]
    halves, _, _, inner = gate_up.shape
    experts = halves // 2
    shard = adapter_weight.shape[0]
    params = pltpu.CompilerParams(vmem_limit_bytes=VMEM_LIMIT)

    def message():
        cache_hit = jnp.any(tile_image[:, None] == cache_ids[None, :], axis=1)
        tokens_own = jnp.where(
            cache_hit[:, None, None], cached_rows.reshape(slots, tile_rows, half_width), activate(tile_hidden)
        ).reshape(toks, half_width)
        flags = jnp.broadcast_to(jnp.where(cache_hit, 0.0, 1.0).astype(BF16)[:, None], (slots, toks))
        info_own = jnp.concatenate([routes.T.astype(BF16), flags, jnp.zeros((16 - TOP - slots, toks), BF16)])
        gates = [jnp.pad(piece, ((0, 16 - TOP), (0, 0))) for piece in split3(route_gates.T)]
        info_own = jnp.concatenate([info_own] + gates, axis=1)
        info_own = jnp.pad(info_own, ((0, 0), (0, half_width - 4 * toks)))
        return jnp.concatenate([tokens_own, info_own])

    def fetch(base, count, limit):
        shape = (count, half_width, 2 * inner)
        return pl.pallas_call(
            functools.partial(fetch_kernel, base),
            in_specs=[ANY],
            out_specs=VM,
            out_shape=jax.ShapeDtypeStruct(shape, BF16),
            scratch_shapes=[
                pltpu.VMEM((count, half_width, 2, inner), BF16),
                pltpu.SemaphoreType.DMA((count,)),
            ],
            compiler_params=pltpu.CompilerParams(vmem_limit_bytes=limit << 20),
            cost_estimate=pl.CostEstimate(
                flops=512 * count * half_width * 2 * inner, bytes_accessed=8 * count * half_width * inner, transcendentals=0
            ),
        )(gate_up)

    near = experts // 2
    far = experts - near
    count = halves // 4
    fetches = [functools.partial(fetch, i * count, count, limit) for i, limit in enumerate(FETCH_LIMITS)]
    part = shard // 2
    weight_part = jnp.where(lax.axis_index("grp") == 0, adapter_weight[:part], adapter_weight[part:])
    weight_ring, sent, fetched, weight_across = ring_gather_two(weight_part, message, fetches)
    weight_in = [adapter_weight, *weight_ring[1:], *weight_across]
    *fetched_near, fetched_far = fetched
    most = NR * CAP
    pre_shape = jax.ShapeDtypeStruct((2 * near, most, 2 * inner), BF16)
    rows, mix, own_near = pl.pallas_call(
        functools.partial(prologue_kernel, experts, slots, tile_rows),
        in_specs=[VM] * (NR + len(weight_in)) + [VM] * len(fetched_near),
        out_specs=[VM, VM, VM],
        out_shape=[
            jax.ShapeDtypeStruct((far, most, half_width), BF16),
            jax.ShapeDtypeStruct((NR, 2, experts * CAP, toks), BF16),
            pre_shape,
        ],
        scratch_shapes=[
            pltpu.VMEM((NR, toks + 16, half_width), BF16),
            pltpu.VMEM((NR * shard, half_width), BF16),
            pltpu.VMEM((NR * slots // 2, tile_rows, half_width), BF16),
            pltpu.VMEM((near, most, half_width), BF16),
            pltpu.SMEM((NR * slots,), jnp.int32),
        ],
        compiler_params=pltpu.CompilerParams(vmem_limit_bytes=VMEM_SMALL),
    )(*sent, *weight_in, *fetched_near)
    other_near = swap(own_near, "narrow")

    own_far = pl.pallas_call(
        functools.partial(first_kernel, 3 * count),
        in_specs=[VM, VM, ANY],
        out_specs=VM,
        out_shape=jax.ShapeDtypeStruct((2 * far, most, 2 * inner), BF16),
        scratch_shapes=[
            pltpu.VMEM((count, half_width, 2, inner), BF16),
            pltpu.VMEM((count // 2, 2 * most, 2 * half_width), BF16),
            pltpu.SemaphoreType.DMA((count,)),
        ],
        compiler_params=pltpu.CompilerParams(vmem_limit_bytes=VMEM_FAR),
        cost_estimate=pl.CostEstimate(
            flops=16 * most * half_width * far * inner, bytes_accessed=8 * far * half_width * inner, transcendentals=0
        ),
    )(rows, fetched_far, gate_up)
    own_far, other_near = tie(own_far, other_near)
    other_far = swap(own_far, "narrow")

    near_pairs = pl.pallas_call(
        second_near_kernel,
        in_specs=[VM, VM, ANY],
        out_specs=VM,
        out_shape=jax.ShapeDtypeStruct((near, most, half_width), BF16),
        scratch_shapes=[pltpu.VMEM((2 * near, inner, half_width), BF16), pltpu.SemaphoreType.DMA((near,))],
        compiler_params=params,
        cost_estimate=pl.CostEstimate(
            flops=4 * near * most * inner * half_width,
            bytes_accessed=4 * near * inner * half_width,
            transcendentals=2 * near * most * inner,
        ),
    )(own_near, other_near, expert_down)
    near_pairs, other_far = tie(near_pairs, other_far)

    n_second = 2
    width = half_width // n_second
    mixed = []
    hidden = None
    for c in range(n_second):
        start = hidden is None
        out = pl.pallas_call(
            functools.partial(second_far_kernel, 2 * near, c, width),
            in_specs=[VM] * (4 if start else 3) + [ANY],
            out_specs=[VM] * (start + NR),
            out_shape=[jax.ShapeDtypeStruct((2 * far, most, inner), BF16)] * start
            + [jax.ShapeDtypeStruct((toks, width), BF16)] * NR,
            scratch_shapes=[
                pltpu.VMEM((far, most, width), BF16),
                pltpu.VMEM((2 * far, inner, width), BF16),
                pltpu.SemaphoreType.DMA((far,)),
            ],
            compiler_params=params,
            cost_estimate=pl.CostEstimate(
                flops=4 * far * most * inner * width, bytes_accessed=4 * far * inner * width, transcendentals=0
            ),
        )(*((own_far, other_far) if start else (hidden,)), near_pairs, mix, expert_down)
        if start:
            hidden, *out = out
        mixed.append(ring_scatter(out, c % 2 == 0))
    return jnp.concatenate(mixed, axis=1)


def solution(mesh):
    body = on_device_ring if mesh.shape["wide"] == NR else on_device_plain
    return jax.shard_map(
        body,
        mesh=mesh,
        in_specs=(
            P(("grp", "wide"), None, None),
            P(("grp", "wide"), "narrow"),
            P(("grp", "wide")),
            P("grp"),
            P("wide", "narrow"),
            P(("grp", "wide"), None),
            P(("grp", "wide"), None),
            P("wide", "narrow", None, None),
            P("wide", None, "narrow"),
        ),
        out_specs=P(("grp", "wide"), "narrow"),
        check_vma=False,
    )
```
